512 devices in a mesh: ctx: 32 (over x_hi, y, core), dp: 16 (over x_lo, z).
Axes of the slice: x: 4 (x_hi: 2, x_lo: 2; x = x_hi * 2 + x_lo), y: 8, z: 8, core: 2. Of those that a mesh axis runs over, the one named last changes fastest.
Arguments:
- out_grad: bfloat16 [16, 4096, 256], P('dp', 'ctx'), may hold values from -0.0234375 to 0.0234375
- gate_out: bfloat16 [16, 4096, 256], P('dp', 'ctx'), may hold values from -6 to 6
- gate_in: bfloat16 [16, 4096, 256], P('dp', 'ctx'), may hold values from -6 to 6
- values: bfloat16 [16, 4096, 256], P('dp', 'ctx'), may hold values from -6 to 6
- doc_tiles: int32 [16, 4], P('dp'), may hold values from 0 to 32, as said below
Outputs:
- kernel_derivative: float32 [4096, 256], P('ctx')
The draws below stay inside these ranges and needn't reach their ends.
Inputs may be any that keep to these rules, and one draw needn't show every extreme that they name: `doc_tiles`: row w lists, in order, the lengths in tiles of the documents of window w; they sum to 32; an entry of 0 stands for no document.
All inputs are finite; a program needn't handle non-finite values.
Results may differ from the reference program's by a relative error of at most 0.0029.
Values may be sent and summed in bfloat16 or wider, within the bound.
A program may use at most 64 MiB of HBM per device.

```python
import jax
import jax.numpy as jnp
from jax import lax

CH = 256
DOCS = 4
SEQ = 4096
WINDOWS = 16
TILES = 32


def draw_doc_tiles(key, part):
    key = jax.random.fold_in(key, 7)
    row_keys = jax.random.split(jax.random.fold_in(key, 1), WINDOWS)

    def one_row(row_key):
        cut_points = jax.random.permutation(row_key, TILES - 1)[:DOCS - 1].astype(jnp.int32) + 1
        bounds = jnp.concatenate([jnp.zeros((1,), jnp.int32), jnp.sort(cut_points), jnp.full((1,), TILES, jnp.int32)])
        return bounds[1:] - bounds[:-1]
    lengths = jax.vmap(one_row)(row_keys)
    whole_row = jax.random.randint(jax.random.fold_in(key, 2), (), 0, WINDOWS)
    single = jnp.concatenate([jnp.full((1,), TILES, jnp.int32), jnp.zeros((DOCS - 1,), jnp.int32)])
    chosen = (jnp.arange(WINDOWS, dtype=jnp.int32) == whole_row)[:, None]
    return jnp.where(chosen, single[None, :], lengths).astype(jnp.int32)


def shard_levels(stream_key, extent, cuts, least, high):
    factor_of = 1.0
    for position, blocks in cuts:
        steps = jax.random.uniform(jax.random.fold_in(jax.random.fold_in(stream_key, 6), position), (blocks,), jnp.float32, least / len(cuts), high / len(cuts))
        factor_of = factor_of * jnp.repeat(jnp.exp(steps), extent[position] // blocks).reshape((-1,) + (1,) * (len(extent) - 1 - position))
    return factor_of


def scatter_about(own_key, extent, scale, reach, cuts=(), held_as=jnp.bfloat16):
    gain = shard_levels(own_key, extent, cuts, -0.22, 0.18) if cuts else 1.0
    result = jax.random.normal(own_key, extent, jnp.float32) * scale * gain
    return jnp.minimum(jnp.maximum(result, -reach), reach).astype(held_as)


def setup_inputs(seed: int = 0) -> dict:
    seeds = jax.random.split(jax.random.key(seed), 6)
    return {
        "out_grad": scatter_about(seeds[0], (WINDOWS, SEQ, CH), (SEQ * WINDOWS) ** -0.5, 0.0234375, ((0, 16), (1, 32))),
        "gate_out": scatter_about(seeds[1], (WINDOWS, SEQ, CH), 1.0, 6.0, ((0, 16), (1, 32))),
        "gate_in": scatter_about(seeds[2], (WINDOWS, SEQ, CH), 1.0, 6.0, ((0, 16), (1, 32))),
        "values": scatter_about(seeds[3], (WINDOWS, SEQ, CH), 1.0, 6.0, ((0, 16), (1, 32))),
        "doc_tiles": draw_doc_tiles(jax.random.fold_in(seeds[5], 71), 0),
    }


tile_width = 128


def block_sequence_labels(lengths, tile_count):
    doc_ends = jnp.cumsum(lengths)
    tile_index = jnp.arange(tile_count, dtype=jnp.int32)
    return jnp.sum((tile_index[:, None] >= doc_ends[None, :]).astype(jnp.int32), axis=1)


def window_gradient(window_data):
    out_grad, gate_out, gate_in, values, lengths = window_data
    length = out_grad.shape[0]
    weighted = gate_out.astype(jnp.float32) * out_grad.astype(jnp.float32)
    gated_input = (gate_in.astype(jnp.float32) * values.astype(jnp.float32)).astype(jnp.bfloat16)
    gated_input = lax.optimization_barrier(gated_input).astype(jnp.float32)
    position_doc = jnp.repeat(block_sequence_labels(lengths, length // tile_width), tile_width)

    def one_document(summed, doc_index):
        doc_mask = (position_doc == doc_index).astype(jnp.float32)[:, None]
        head_hat = jnp.fft.rfft(weighted * doc_mask, n=2 * length, axis=0)
        tail_hat = jnp.fft.rfft(gated_input * doc_mask, n=2 * length, axis=0)
        correlation = jnp.fft.irfft(head_hat * jnp.conj(tail_hat), n=2 * length, axis=0)[:length]
        return summed + correlation, None

    initial = jnp.zeros((length, out_grad.shape[1]), jnp.float32)
    summed, _ = lax.scan(one_document, initial, jnp.arange(DOCS, dtype=jnp.int32))
    return summed


def reference(out_grad, gate_out, gate_in, values, doc_tiles):
    def one_window(summed, window_data):
        return summed + window_gradient(window_data), None

    initial = jnp.zeros((SEQ, CH), jnp.float32)
    summed, _ = lax.scan(one_window, initial, (out_grad, gate_out, gate_in, values, doc_tiles))
    return summed
```

```python
import functools

import jax
import jax.numpy as jnp
import numpy as np
from jax import lax
from jax.experimental import pallas as pl
from jax.experimental.pallas import tpu as pltpu
from jax.sharding import PartitionSpec as P

TILE = 128
ROWS = 8
MESH = pl.DeviceIdType.MESH


def transform_tables():
    positions = np.arange(TILE)
    theta = 2.0 * np.pi * (np.arange(TILE) + 0.5) / (2 * TILE)
    forward = np.concatenate(
        [np.cos(positions[:, None] * theta), -np.sin(positions[:, None] * theta)], axis=1
    )
    inverse = np.concatenate(
        [np.cos(theta[:, None] * positions), -np.sin(theta[:, None] * positions)], axis=0
    )
    inverse = inverse / TILE
    pair = []
    for table in (forward, inverse):
        table = table.astype(np.float32)
        high = table.astype(jnp.bfloat16)
        low = (table - high.astype(np.float32)).astype(jnp.bfloat16)
        pair.append(np.stack([high, low]))
    return pair


def product(left, right):
    return jnp.dot(left, right, preferred_element_type=jnp.float32)


def kernel(
    members, windows, out_grad, gate_out, gate_in, values, doc_tiles, forward, inverse, out,
    outgoing, incoming, docs, spectra, sums, lags, parts, total, landing,
    send_sems, recv_sems,
):
    me = lax.axis_index("ctx")
    window = lax.axis_index("dp")
    per_owner = members // windows
    channels = members * ROWS

    barrier = pltpu.get_barrier_semaphore()
    for step in range(1, members):
        pl.semaphore_signal(
            barrier, 1, device_id={"ctx": lax.rem(me + step, members)}, device_id_type=MESH
        )
    for step in range(1, windows):
        pl.semaphore_signal(
            barrier, 1, device_id={"dp": lax.rem(window + step, windows)}, device_id_type=MESH
        )

    with jax.named_scope("gate"):
        weighted = gate_out[0].astype(jnp.float32) * out_grad[0].astype(jnp.float32)
        gated = gate_in[0].astype(jnp.float32) * values[0].astype(jnp.float32)
        weighted = weighted.T.reshape(members, 1, ROWS, TILE)
        gated = gated.T.reshape(members, 1, ROWS, TILE)
        outgoing[...] = (
            jnp.concatenate([weighted, gated], axis=1)
            .reshape(members, 2 * ROWS, TILE)
            .astype(jnp.bfloat16)
        )
        incoming[me] = outgoing[me]

        tile = lax.broadcasted_iota(jnp.int32, docs.shape, 0)
        label = jnp.zeros(docs.shape, jnp.float32)
        end = jnp.int32(0)
        for entry in range(doc_tiles.shape[1]):
            end = end + doc_tiles[0, entry]
            label += (tile >= end).astype(jnp.float32)
        docs[...] = label

    with jax.named_scope("enter"):
        pl.semaphore_wait(barrier, members + windows - 2)

    with jax.named_scope("send_tiles"):
        for step in range(1, members):
            peer = lax.rem(me + step, members)
            pltpu.make_async_remote_copy(
                src_ref=outgoing.at[peer],
                dst_ref=incoming.at[me],
                send_sem=send_sems.at[0],
                recv_sem=recv_sems.at[0],
                device_id={"ctx": peer},
                device_id_type=MESH,
            ).start()
        others = pl.ds(0, members - 1)
        pltpu.make_async_copy(outgoing.at[others], outgoing.at[others], send_sems.at[0]).wait()
        pltpu.make_async_copy(incoming.at[others], incoming.at[others], recv_sems.at[0]).wait()

    with jax.named_scope("transform"):
        tiles = incoming[...].reshape(members * 2 * ROWS, TILE)
        hats = product(tiles, forward[0]) + product(tiles, forward[1])
        spectra[pl.ds(0, members)] = hats.reshape(members, 2 * ROWS, 2 * TILE)
        spectra[pl.ds(members, ROWS)] = jnp.zeros((ROWS, 2 * ROWS, 2 * TILE), jnp.float32)

    with jax.named_scope("pairs"):
        for first in range(0, members, ROWS):

            def lag_block(offset, carried, first=first):
                lag = first + offset
                real = jnp.zeros((ROWS, TILE), jnp.float32)
                imag = jnp.zeros((ROWS, TILE), jnp.float32)
                for source in range(members - first):
                    head = source + lag
                    head_real = spectra[head, :ROWS, :TILE]
                    head_imag = spectra[head, :ROWS, TILE:]
                    tail_real = spectra[source, ROWS:, :TILE]
                    tail_imag = spectra[source, ROWS:, TILE:]
                    same = docs[head] == docs[source]
                    real += jnp.where(same, head_real * tail_real + head_imag * tail_imag, 0.0)
                    imag += jnp.where(same, head_imag * tail_real - head_real * tail_imag, 0.0)
                sums[lag, :, :TILE] = real
                sums[lag, :, TILE:] = imag
                return carried

            lax.fori_loop(0, min(ROWS, members - first), lag_block, 0)
        sums[members] = jnp.zeros((ROWS, 2 * TILE), jnp.float32)

    with jax.named_scope("back"):
        here = sums[pl.ds(0, members)].reshape(members * ROWS, 2 * TILE)
        after = sums[pl.ds(1, members)].reshape(members * ROWS, 2 * TILE)
        parity = lax.broadcasted_iota(jnp.int32, (members * ROWS, TILE), 1) % 2
        sign = (1 - 2 * parity).astype(jnp.float32)
        both = jnp.concatenate(
            [here[:, :TILE] + sign * after[:, TILE:], here[:, TILE:] - sign * after[:, :TILE]], axis=1
        )
        high = both.astype(jnp.bfloat16)
        low = (both - high.astype(jnp.float32)).astype(jnp.bfloat16)
        result = product(high, inverse[0]) + product(low, inverse[0]) + product(high, inverse[1])
        lags[...] = result.reshape(lags.shape).astype(lags.dtype)
        parts[window] = lags[window]

    with jax.named_scope("send_lags"):
        for step in range(1, windows):
            peer = lax.rem(window + step, windows)
            pltpu.make_async_remote_copy(
                src_ref=lags.at[peer],
                dst_ref=parts.at[window],
                send_sem=send_sems.at[1],
                recv_sem=recv_sems.at[1],
                device_id={"dp": peer},
                device_id_type=MESH,
            ).start()
        others = pl.ds(0, windows - 1)
        pltpu.make_async_copy(lags.at[others], lags.at[others], send_sems.at[1]).wait()
        pltpu.make_async_copy(parts.at[others], parts.at[others], recv_sems.at[1]).wait()
        total[...] = jnp.sum(parts[...].astype(jnp.float32), axis=0).reshape(total.shape)

    with jax.named_scope("spread"):
        for step in range(windows):
            reader = lax.rem(window + step, windows)
            for block in range(per_owner):
                lag = window * per_owner + block
                own = (reader == window) & (lag == me)

                @pl.when(own)
                def _():
                    pltpu.make_async_copy(total.at[block], landing.at[me], recv_sems.at[2]).start()

                @pl.when(jnp.logical_not(own))
                def _():
                    pltpu.make_async_remote_copy(
                        src_ref=total.at[block],
                        dst_ref=landing.at[me],
                        send_sem=send_sems.at[2],
                        recv_sem=recv_sems.at[2],
                        device_id={"ctx": lag, "dp": reader},
                        device_id_type=MESH,
                    ).start()

        keeps = me // per_owner == window
        count = windows * per_owner
        span = landing.at[pl.ds(0, count)]
        fewer = landing.at[pl.ds(0, count - 1)]

        @pl.when(keeps)
        def _():
            pltpu.make_async_copy(fewer, fewer, send_sems.at[2]).wait()

        @pl.when(jnp.logical_not(keeps))
        def _():
            pltpu.make_async_copy(span, span, send_sems.at[2]).wait()

        pltpu.make_async_copy(landing, landing, recv_sems.at[2]).wait()

    out[...] = landing[...].reshape(channels, TILE).T


def per_device(members, windows, forward, inverse, *arrays):
    channels = members * ROWS
    per_owner = members // windows
    vmem = pl.BlockSpec(memory_space=pltpu.VMEM)
    smem = pl.BlockSpec(memory_space=pltpu.SMEM)
    return pl.pallas_call(
        functools.partial(kernel, members, windows),
        out_shape=jax.ShapeDtypeStruct((TILE, channels), jnp.float32),
        in_specs=[vmem] * 4 + [smem] + [vmem] * 2,
        out_specs=vmem,
        scratch_shapes=[
            pltpu.VMEM((members, 2 * ROWS, TILE), jnp.bfloat16),
            pltpu.VMEM((members, 2 * ROWS, TILE), jnp.bfloat16),
            pltpu.VMEM((members + ROWS, ROWS, TILE), jnp.float32),
            pltpu.VMEM((members + ROWS, 2 * ROWS, 2 * TILE), jnp.float32),
            pltpu.VMEM((members + 1, ROWS, 2 * TILE), jnp.float32),
            pltpu.VMEM((windows, per_owner * ROWS, TILE), jnp.float32),
            pltpu.VMEM((windows, per_owner * ROWS, TILE), jnp.float32),
            pltpu.VMEM((per_owner, ROWS, TILE), jnp.float32),
            pltpu.VMEM((members, ROWS, TILE), jnp.float32),
            pltpu.SemaphoreType.DMA((3,)),
            pltpu.SemaphoreType.DMA((3,)),
        ],
        compiler_params=pltpu.CompilerParams(
            collective_id=0, has_side_effects=True, vmem_limit_bytes=32 * 1024 * 1024
        ),
    )(*arrays, forward, inverse)


def solution(mesh):
    members, windows = mesh.shape["ctx"], mesh.shape["dp"]
    forward, inverse = transform_tables()

    def run(*arrays):
        return per_device(members, windows, jnp.asarray(forward), jnp.asarray(inverse), *arrays)

    return jax.shard_map(
        run,
        mesh=mesh,
        in_specs=(P("dp", "ctx", None),) * 4 + (P("dp", None),),
        out_specs=P("ctx", None),
        check_vma=False,
    )
```

```python
import functools

import jax
import jax.numpy as jnp
import numpy as np
from jax import lax
from jax.experimental import pallas as pl
from jax.experimental.pallas import tpu as pltpu
from jax.sharding import PartitionSpec as P

TILE = 128
ROWS = 8
MESH = pl.DeviceIdType.MESH


def transform_tables():
    positions = np.arange(TILE)
    theta = 2.0 * np.pi * (np.arange(TILE) + 0.5) / (2 * TILE)
    forward = np.concatenate(
        [np.cos(positions[:, None] * theta), -np.sin(positions[:, None] * theta)], axis=1
    )
    inverse = np.concatenate(
        [np.cos(theta[:, None] * positions), -np.sin(theta[:, None] * positions)], axis=0
    )
    inverse = inverse / TILE
    split = []
    for table in (forward, inverse):
        table = table.astype(np.float32)
        high = table.astype(jnp.bfloat16)
        split += [high, (table - high.astype(np.float32)).astype(jnp.bfloat16)]
    return split


def product(left, right):
    return jnp.dot(left, right, preferred_element_type=jnp.float32)


def wrap(index, size):
    return lax.rem(index + 8 * size, size)


def owner_of(lag, member, ring):
    slot, row, low = lag // (2 * ring), lag // 2 % ring, lag % 2
    gap = row - member // 2 % ring
    core = member % 2
    if slot == 0:
        depth = jnp.where(core == 0, gap, 5 - gap)
    else:
        depth = jnp.where(core == 0, 1 - gap, gap - 4)
    return low * ring + wrap(depth, ring)


def lag_of(window, member, slot, ring):
    low, depth = window // ring, window % ring
    core = member % 2
    if slot == 0:
        gap = jnp.where(core == 0, depth, 5 - depth)
    else:
        gap = jnp.where(core == 0, 1 - depth, depth + 4)
    row = wrap(member // 2 % ring + gap, ring)
    return (slot * ring + row) * 2 + low


def remote(source, target, send_sem, recv_sem, **place):
    return pltpu.make_async_remote_copy(
        src_ref=source, dst_ref=target, send_sem=send_sem, recv_sem=recv_sem,
        device_id=place, device_id_type=MESH,
    )


def wait_bytes(ref, sem):
    pltpu.make_async_copy(ref, ref, sem).wait()


def kernel(
    members, windows, out_grad, gate_out, gate_in, values, doc_tiles, fwd_high, fwd_low, inv_high, inv_low, out,
    og, go, gi, va, lengths, fwd, inv,
    outgoing, incoming, docs, spectra, sums, lags, parts, total, landing,
    load_sems, tile_send, tile_recv, lag_send, lag_recv, last_send, last_recv,
):
    me = lax.axis_index("ctx")
    window = lax.axis_index("dp")
    ring = windows // 2
    channels = members * ROWS
    my_half, my_row, my_core = me // (2 * ring), me // 2 % ring, me % 2

    def member_at(half, row, core):
        return (lax.rem(my_half + half, 2) * ring + lax.rem(my_row + row, ring)) * 2 + lax.rem(
            my_core + core, 2
        )

    gaps = [[0] + ([1, ring - 1] if ring > 2 else [1])]
    gaps += [[gap, ring - gap] for gap in range(2, ring // 2)]
    gaps += [[ring // 2]] if ring > 2 else []
    groups = [
        [(half, gap, core) for gap in group for half in (1, 0) for core in (0, 1) if half + gap + core]
        for group in gaps
    ]
    far_first = [place for group in reversed(groups) for place in reversed(group)]

    barrier = pltpu.get_barrier_semaphore()
    for place in far_first:
        pl.semaphore_signal(barrier, 1, device_id={"ctx": member_at(*place)}, device_id_type=MESH)
    for step in range(1, windows):
        pl.semaphore_signal(
            barrier, 1, device_id={"dp": lax.rem(window + step, windows)}, device_id_type=MESH
        )
    pairs = [
        (out_grad, og), (gate_out, go), (gate_in, gi), (values, va), (doc_tiles, lengths),
        (fwd_high, fwd.at[pl.ds(0, TILE)]), (fwd_low, fwd.at[pl.ds(TILE, TILE)]),
        (inv_high, inv.at[0]), (inv_low, inv.at[1]),
    ]
    loads = [
        pltpu.make_async_copy(source, target, load_sems.at[n]) for n, (source, target) in enumerate(pairs)
    ]
    for load in loads:
        load.start()
    for load in loads:
        load.wait()

    weighted = go[0].astype(jnp.float32) * og[0].astype(jnp.float32)
    gated = gi[0].astype(jnp.float32) * va[0].astype(jnp.float32)
    weighted = weighted.T.reshape(members, 1, ROWS, TILE)
    gated = gated.T.reshape(members, 1, ROWS, TILE)
    outgoing[...] = (
        jnp.concatenate([weighted, gated], axis=1)
        .reshape(members, 2 * ROWS, TILE)
        .astype(jnp.bfloat16)
    )
    incoming[me] = outgoing[me]

    tile = lax.broadcasted_iota(jnp.int32, docs.shape, 0)
    label = jnp.zeros(docs.shape, jnp.float32)
    end = jnp.int32(0)
    for entry in range(lengths.shape[1]):
        end = end + lengths[0, entry]
        label += (tile >= end).astype(jnp.float32)
    docs[...] = label
    spectra[pl.ds(members, ROWS)] = jnp.zeros((ROWS, 2 * ROWS, 2 * TILE), jnp.float32)
    sums[members] = jnp.zeros((ROWS, 2 * TILE), jnp.float32)

    pl.semaphore_wait(barrier, members + windows - 2)

    for number in reversed(range(len(groups))):
        for place in reversed(groups[number]):
            peer = member_at(*place)
            remote(
                outgoing.at[peer], incoming.at[me], tile_send, tile_recv.at[number], ctx=peer
            ).start()
    for number, group in enumerate(groups):
        wait_bytes(incoming.at[pl.ds(0, len(group))], tile_recv.at[number])
        places = sorted({(half, gap) for half, gap, _ in group})
        if number == 0:
            places = sorted(set(places) | {(0, 0)})
        starts = [
            (lax.rem(my_half + half, 2) * ring + lax.rem(my_row + gap, ring)) * 2 for half, gap in places
        ]
        tiles = jnp.concatenate(
            [incoming[pl.ds(start, 2)].reshape(4 * ROWS, TILE) for start in starts], axis=0
        )
        hats = product(jnp.concatenate([tiles, tiles], axis=1), fwd[...])
        for number_, start in enumerate(starts):
            spectra[pl.ds(start, 2)] = hats[number_ * 4 * ROWS : (number_ + 1) * 4 * ROWS].reshape(
                2, 2 * ROWS, 2 * TILE
            )

    def add_pairs(first, stop, terms):
        def lag_block(lag, carried):
            real = jnp.zeros((ROWS, TILE), jnp.float32)
            imag = jnp.zeros((ROWS, TILE), jnp.float32)
            for source in range(terms):
                head = source + lag
                head_real = spectra[head, :ROWS, :TILE]
                head_imag = spectra[head, :ROWS, TILE:]
                tail_real = spectra[source, ROWS:, :TILE]
                tail_imag = spectra[source, ROWS:, TILE:]
                same = docs[head] == docs[source]
                real += jnp.where(same, head_real * tail_real + head_imag * tail_imag, 0.0)
                imag += jnp.where(same, head_imag * tail_real - head_real * tail_imag, 0.0)
            sums[lag, :, :TILE] = real
            sums[lag, :, TILE:] = imag
            return carried

        lax.fori_loop(first, stop, lag_block, 0)

    parity = lax.broadcasted_iota(jnp.int32, (members // 2 * ROWS, TILE), 1) % 2
    sign = (1 - 2 * parity).astype(jnp.float32)

    def back_and_send(slot):
        half = members // 2
        here = sums[pl.ds(slot * half, half)].reshape(half * ROWS, 2 * TILE)
        after = sums[pl.ds(slot * half + 1, half)].reshape(half * ROWS, 2 * TILE)
        both = jnp.concatenate(
            [here[:, :TILE] + sign * after[:, TILE:], here[:, TILE:] - sign * after[:, :TILE]], axis=1
        )
        high = both.astype(jnp.bfloat16)
        low = (both - high.astype(jnp.float32)).astype(jnp.bfloat16)
        result = product(high, inv[0]) + product(low, inv[0]) + product(high, inv[1])
        lags[pl.ds(slot * half, half)] = result.reshape(half, ROWS, TILE)
        for lag in range(slot * half, (slot + 1) * half):
            owner = owner_of(lag, me, ring)

            @pl.when(owner != window)
            def _():
                remote(
                    lags.at[lag], parts.at[slot, window], lag_send, lag_recv.at[slot], dp=owner
                ).start()

        parts[slot, window] = lags[lag_of(window, me, slot, ring)]

    half = members // 2
    quarter = members // 4
    add_pairs(0, quarter, members)
    add_pairs(quarter, half + 1, members - quarter)
    back_and_send(0)
    add_pairs(half + 1, half + quarter, half)
    add_pairs(half + quarter, members, quarter)
    back_and_send(1)

    others = pl.ds(0, windows - 1)
    for slot in range(2):
        wait_bytes(parts.at[slot, others], lag_recv.at[slot])
        total[slot] = jnp.sum(parts[slot], axis=0)
        lag = lag_of(window, me, slot, ring)
        for depth in range(ring):
            for low in range(2):
                reader = low * ring + depth
                own = (reader == window) & (lag == me)

                @pl.when(own)
                def _():
                    pltpu.make_async_copy(total.at[slot], landing.at[me], last_recv).start()

                @pl.when(jnp.logical_not(own))
                def _():
                    remote(
                        total.at[slot], landing.at[me], last_send, last_recv, ctx=lag, dp=reader
                    ).start()

    wait_bytes(landing, last_recv)
    out[...] = landing[...].reshape(channels, TILE).T

    wait_bytes(outgoing.at[pl.ds(0, members - 1)], tile_send)
    wait_bytes(lags.at[pl.ds(0, members - 2)], lag_send)
    keeps = (lag_of(window, me, 0, ring) == me) | (lag_of(window, me, 1, ring) == me)

    @pl.when(keeps)
    def _():
        wait_bytes(landing.at[pl.ds(0, members - 1)], last_send)

    @pl.when(jnp.logical_not(keeps))
    def _():
        wait_bytes(landing, last_send)


def per_device(members, windows, tables, *arrays):
    channels = members * ROWS
    hbm = pl.BlockSpec(memory_space=pltpu.HBM)
    return pl.pallas_call(
        functools.partial(kernel, members, windows),
        out_shape=pltpu.VMEM((TILE, channels), jnp.float32),
        in_specs=[hbm] * 9,
        out_specs=pl.BlockSpec(memory_space=pltpu.VMEM),
        scratch_shapes=[
            pltpu.VMEM((1, TILE, channels), jnp.bfloat16),
            pltpu.VMEM((1, TILE, channels), jnp.bfloat16),
            pltpu.VMEM((1, TILE, channels), jnp.bfloat16),
            pltpu.VMEM((1, TILE, channels), jnp.bfloat16),
            pltpu.SMEM(arrays[4].shape, jnp.int32),
            pltpu.VMEM((2 * TILE, 2 * TILE), jnp.bfloat16),
            pltpu.VMEM((2, 2 * TILE, TILE), jnp.bfloat16),
            pltpu.VMEM((members, 2 * ROWS, TILE), jnp.bfloat16),
            pltpu.VMEM((members, 2 * ROWS, TILE), jnp.bfloat16),
            pltpu.VMEM((members + ROWS, ROWS, TILE), jnp.float32),
            pltpu.VMEM((members + ROWS, 2 * ROWS, 2 * TILE), jnp.float32),
            pltpu.VMEM((members + 1, ROWS, 2 * TILE), jnp.float32),
            pltpu.VMEM((members, ROWS, TILE), jnp.float32),
            pltpu.VMEM((2, windows, ROWS, TILE), jnp.float32),
            pltpu.VMEM((2, ROWS, TILE), jnp.float32),
            pltpu.VMEM((members, ROWS, TILE), jnp.float32),
            pltpu.SemaphoreType.DMA((9,)),
            pltpu.SemaphoreType.DMA,
            pltpu.SemaphoreType.DMA((4,)),
            pltpu.SemaphoreType.DMA,
            pltpu.SemaphoreType.DMA((2,)),
            pltpu.SemaphoreType.DMA,
            pltpu.SemaphoreType.DMA,
        ],
        compiler_params=pltpu.CompilerParams(
            collective_id=0, has_side_effects=True, vmem_limit_bytes=60 * 1024 * 1024
        ),
    )(*[pltpu.with_memory_space_constraint(array, pltpu.HBM) for array in (*arrays, *tables)])


def solution(mesh):
    members, windows = mesh.shape["ctx"], mesh.shape["dp"]
    tables = transform_tables()

    def run(*arrays):
        return per_device(members, windows, [jnp.asarray(table) for table in tables], *arrays)

    return jax.shard_map(
        run,
        mesh=mesh,
        in_specs=(P("dp", "ctx", None),) * 4 + (P("dp", None),),
        out_specs=P("ctx", None),
        check_vma=False,
    )
```

```python
import functools

import jax
import jax.numpy as jnp
import numpy as np
from jax import lax
from jax.experimental import pallas as pl
from jax.experimental.pallas import tpu as pltpu
from jax.sharding import PartitionSpec as P

TILE = 128
ROWS = 8
MESH = pl.DeviceIdType.MESH


def transform_tables():
    positions = np.arange(TILE)
    theta = 2.0 * np.pi * (np.arange(TILE) + 0.5) / (2 * TILE)
    forward = np.concatenate(
        [np.cos(positions[:, None] * theta), -np.sin(positions[:, None] * theta)], axis=1
    )
    inverse = np.concatenate(
        [np.cos(theta[:, None] * positions), -np.sin(theta[:, None] * positions)], axis=0
    )
    inverse = inverse / TILE
    split = []
    for table in (forward, inverse):
        table = table.astype(np.float32)
        high = table.astype(jnp.bfloat16)
        split += [high, (table - high.astype(np.float32)).astype(jnp.bfloat16)]
    return split


def product(left, right):
    return jnp.dot(left, right, preferred_element_type=jnp.float32)


def wrap(index, size):
    return lax.rem(index + 8 * size, size)


PLAN = [
    [[3, 1, 0, 6, 5, 4, 2, 7], [1, 6, 5, 0, 4, 2, 3, 7], [2, 3, 6, 4, 0, 1, 5, 7], [7, 1, 3, 5, 0, 4, 6, 2]],
    [[6, 2, 3, 0, 5, 4, 7, 1], [2, 5, 1, 0, 4, 7, 6, 3], [7, 3, 4, 6, 0, 5, 1, 2], [2, 0, 7, 4, 6, 1, 3, 5]],
    [[3, 2, 0, 5, 6, 7, 1, 4], [5, 7, 6, 1, 3, 0, 2, 4], [4, 3, 0, 7, 1, 2, 5, 6], [1, 7, 0, 5, 6, 3, 4, 2]],
    [[7, 5, 2, 1, 6, 3, 4, 0], [6, 7, 5, 2, 1, 3, 0, 4], [3, 4, 5, 2, 1, 7, 6, 0], [7, 5, 4, 1, 2, 6, 0, 3]],
    [[1, 2, 7, 3, 4, 6, 5, 0], [4, 1, 2, 3, 7, 5, 6, 0], [0, 2, 6, 7, 3, 1, 4, 5], [0, 6, 2, 7, 4, 1, 3, 5]],
    [[5, 4, 2, 7, 3, 6, 1, 0], [5, 0, 7, 4, 3, 2, 1, 6], [0, 1, 5, 4, 7, 6, 2, 3], [2, 6, 5, 7, 3, 4, 0, 1]],
    [[1, 0, 4, 5, 7, 2, 3, 6], [4, 7, 1, 6, 5, 0, 2, 3], [6, 4, 2, 3, 7, 0, 5, 1], [3, 5, 1, 6, 4, 0, 7, 2]],
    [[5, 6, 7, 2, 1, 3, 0, 4], [6, 0, 4, 3, 2, 5, 1, 7], [4, 3, 0, 2, 1, 6, 7, 5], [0, 4, 3, 1, 2, 7, 5, 6]],
]


def row_codes(ring):
    plan = PLAN if ring == 8 else [[[(y + z) % ring for z in range(ring)] for _ in range(4)] for y in range(ring)]
    return [
        [[sum(plan[y][2 * slot + core][z] << 3 * y for y in range(ring)) for z in range(ring)] for core in range(2)]
        for slot in range(2)
    ]


def lag_at(depth, low, member, slot, ring):
    codes = row_codes(ring)[slot]
    code = jnp.where(member % 2 == 0, codes[0][depth], codes[1][depth])
    row = jnp.bitwise_and(jnp.right_shift(code, 3 * (member // 2 % ring)), 7)
    return (slot * ring + row) * 2 + low


def lag_of(window, member, slot, ring):
    lag = lag_at(0, window // ring, member, slot, ring)
    for depth in range(1, ring):
        lag = jnp.where(window % ring == depth, lag_at(depth, window // ring, member, slot, ring), lag)
    return lag


def remote(source, target, send_sem, recv_sem, **place):
    return pltpu.make_async_remote_copy(
        src_ref=source, dst_ref=target, send_sem=send_sem, recv_sem=recv_sem,
        device_id=place, device_id_type=MESH,
    )


def wait_bytes(ref, sem):
    pltpu.make_async_copy(ref, ref, sem).wait()


def kernel(
    members, windows, out_grad, gate_out, gate_in, values, doc_tiles, fwd_high, fwd_low, inv_high, inv_low, out,
    og, go, gi, va, lengths, fwd, inv,
    outgoing, incoming, docs, spectra, sums, lags, parts, total, landing,
    load_sems, tile_send, tile_recv, lag_send, lag_recv, last_send, last_recv,
):
    me = lax.axis_index("ctx")
    window = lax.axis_index("dp")
    ring = windows // 2
    channels = members * ROWS
    my_half, my_row, my_core = me // (2 * ring), me // 2 % ring, me % 2

    def member_at(half, row, core):
        return (lax.rem(my_half + half, 2) * ring + lax.rem(my_row + row, ring)) * 2 + lax.rem(
            my_core + core, 2
        )

    gaps = [[0] + ([1, ring - 1] if ring > 2 else [1])]
    gaps += [[gap, ring - gap] for gap in range(2, ring // 2)]
    gaps += [[ring // 2]] if ring > 2 else []
    groups = [
        [(half, gap, core) for gap in group for half in (1, 0) for core in (0, 1) if half + gap + core]
        for group in gaps
    ]
    far_first = [place for group in reversed(groups) for place in reversed(group)]

    barrier = pltpu.get_barrier_semaphore()
    for place in far_first:
        pl.semaphore_signal(barrier, 1, device_id={"ctx": member_at(*place)}, device_id_type=MESH)
    for step in range(1, windows):
        pl.semaphore_signal(
            barrier, 1, device_id={"dp": lax.rem(window + step, windows)}, device_id_type=MESH
        )
    pairs = [
        (out_grad, og), (gate_out, go), (gate_in, gi), (values, va), (doc_tiles, lengths),
        (fwd_high, fwd.at[pl.ds(0, TILE)]), (fwd_low, fwd.at[pl.ds(TILE, TILE)]),
        (inv_high, inv.at[0]), (inv_low, inv.at[1]),
    ]
    loads = [
        pltpu.make_async_copy(source, target, load_sems.at[n]) for n, (source, target) in enumerate(pairs)
    ]
    for load in loads:
        load.start()
    for load in loads:
        load.wait()

    weighted = go[0].astype(jnp.float32) * og[0].astype(jnp.float32)
    gated = gi[0].astype(jnp.float32) * va[0].astype(jnp.float32)
    weighted = weighted.T.reshape(members, 1, ROWS, TILE)
    gated = gated.T.reshape(members, 1, ROWS, TILE)
    outgoing[...] = (
        jnp.concatenate([weighted, gated], axis=1)
        .reshape(members, 2 * ROWS, TILE)
        .astype(jnp.bfloat16)
    )
    incoming[me] = outgoing[me]

    tile = lax.broadcasted_iota(jnp.int32, docs.shape, 0)
    label = jnp.zeros(docs.shape, jnp.float32)
    end = jnp.int32(0)
    for entry in range(lengths.shape[1]):
        end = end + lengths[0, entry]
        label += (tile >= end).astype(jnp.float32)
    docs[...] = label
    spectra[pl.ds(members, ROWS)] = jnp.zeros((ROWS, 2 * ROWS, 2 * TILE), jnp.float32)
    sums[members] = jnp.zeros((ROWS, 2 * TILE), jnp.float32)

    pl.semaphore_wait(barrier, members + windows - 2)

    late_rows = sorted(range(ring), key=lambda row: min(row, ring - row), reverse=True)
    late_first = [(row, half, core) for row in late_rows for half in range(2) for core in range(2)]
    for row, half, core in late_first:
        peer = (half * ring + row) * 2 + core
        gap = wrap(row - my_row, ring)
        number = jnp.maximum(jnp.minimum(gap, ring - gap) - 1, 0)

        @pl.when(peer != me)
        def _():
            remote(
                outgoing.at[peer], incoming.at[me], tile_send, tile_recv.at[number], ctx=peer
            ).start()

    for number, group in enumerate(groups):
        wait_bytes(incoming.at[pl.ds(0, len(group))], tile_recv.at[number])
        places = sorted({(half, gap) for half, gap, _ in group})
        if number == 0:
            places = sorted(set(places) | {(0, 0)})
        starts = [
            (lax.rem(my_half + half, 2) * ring + lax.rem(my_row + gap, ring)) * 2 for half, gap in places
        ]
        tiles = jnp.concatenate(
            [incoming[pl.ds(start, 2)].reshape(4 * ROWS, TILE) for start in starts], axis=0
        )
        hats = product(jnp.concatenate([tiles, tiles], axis=1), fwd[...])
        for number_, start in enumerate(starts):
            spectra[pl.ds(start, 2)] = hats[number_ * 4 * ROWS : (number_ + 1) * 4 * ROWS].reshape(
                2, 2 * ROWS, 2 * TILE
            )

    def add_pairs(first, stop, terms):
        def lag_block(lag, carried):
            real = jnp.zeros((ROWS, TILE), jnp.float32)
            imag = jnp.zeros((ROWS, TILE), jnp.float32)
            for source in range(terms):
                head = source + lag
                head_real = spectra[head, :ROWS, :TILE]
                head_imag = spectra[head, :ROWS, TILE:]
                tail_real = spectra[source, ROWS:, :TILE]
                tail_imag = spectra[source, ROWS:, TILE:]
                same = docs[head] == docs[source]
                real += jnp.where(same, head_real * tail_real + head_imag * tail_imag, 0.0)
                imag += jnp.where(same, head_imag * tail_real - head_real * tail_imag, 0.0)
            sums[lag, :, :TILE] = real
            sums[lag, :, TILE:] = imag
            return carried

        lax.fori_loop(first, stop, lag_block, 0)

    parity = lax.broadcasted_iota(jnp.int32, (members // 2 * ROWS, TILE), 1) % 2
    sign = (1 - 2 * parity).astype(jnp.float32)

    def back_and_send(slot):
        half = members // 2
        here = sums[pl.ds(slot * half, half)].reshape(half * ROWS, 2 * TILE)
        after = sums[pl.ds(slot * half + 1, half)].reshape(half * ROWS, 2 * TILE)
        both = jnp.concatenate(
            [here[:, :TILE] + sign * after[:, TILE:], here[:, TILE:] - sign * after[:, :TILE]], axis=1
        )
        high = both.astype(jnp.bfloat16)
        low = (both - high.astype(jnp.float32)).astype(jnp.bfloat16)
        result = product(high, inv[0]) + product(low, inv[0]) + product(high, inv[1])
        lags[pl.ds(slot * half, half)] = result.reshape(half, ROWS, TILE)
        for depth in late_rows:
            for low in range(2):
                owner = low * ring + depth

                @pl.when(owner != window)
                def _():
                    remote(
                        lags.at[lag_at(depth, low, me, slot, ring)], parts.at[slot, window],
                        lag_send, lag_recv.at[slot], dp=owner,
                    ).start()

        parts[slot, window] = lags[lag_of(window, me, slot, ring)]

    half = members // 2
    quarter = members // 4
    add_pairs(0, quarter, members)
    add_pairs(quarter, half + 1, members - quarter)
    back_and_send(0)
    add_pairs(half + 1, half + quarter, half)
    add_pairs(half + quarter, members, quarter)
    back_and_send(1)

    others = pl.ds(0, windows - 1)
    for slot in range(2):
        wait_bytes(parts.at[slot, others], lag_recv.at[slot])
        total[slot] = jnp.sum(parts[slot], axis=0)
        lag = lag_of(window, me, slot, ring)
        for depth in range(ring):
            for low in range(2):
                reader = low * ring + depth
                own = (reader == window) & (lag == me)

                @pl.when(own)
                def _():
                    pltpu.make_async_copy(total.at[slot], landing.at[me], last_recv).start()

                @pl.when(jnp.logical_not(own))
                def _():
                    remote(
                        total.at[slot], landing.at[me], last_send, last_recv, ctx=lag, dp=reader
                    ).start()

    wait_bytes(landing, last_recv)
    out[...] = landing[...].reshape(channels, TILE).T

    wait_bytes(outgoing.at[pl.ds(0, members - 1)], tile_send)
    wait_bytes(lags.at[pl.ds(0, members - 2)], lag_send)
    keeps = (lag_of(window, me, 0, ring) == me) | (lag_of(window, me, 1, ring) == me)

    @pl.when(keeps)
    def _():
        wait_bytes(landing.at[pl.ds(0, members - 1)], last_send)

    @pl.when(jnp.logical_not(keeps))
    def _():
        wait_bytes(landing, last_send)


def per_device(members, windows, tables, *arrays):
    channels = members * ROWS
    hbm = pl.BlockSpec(memory_space=pltpu.HBM)
    return pl.pallas_call(
        functools.partial(kernel, members, windows),
        out_shape=pltpu.VMEM((TILE, channels), jnp.float32),
        in_specs=[hbm] * 9,
        out_specs=pl.BlockSpec(memory_space=pltpu.VMEM),
        scratch_shapes=[
            pltpu.VMEM((1, TILE, channels), jnp.bfloat16),
            pltpu.VMEM((1, TILE, channels), jnp.bfloat16),
            pltpu.VMEM((1, TILE, channels), jnp.bfloat16),
            pltpu.VMEM((1, TILE, channels), jnp.bfloat16),
            pltpu.SMEM(arrays[4].shape, jnp.int32),
            pltpu.VMEM((2 * TILE, 2 * TILE), jnp.bfloat16),
            pltpu.VMEM((2, 2 * TILE, TILE), jnp.bfloat16),
            pltpu.VMEM((members, 2 * ROWS, TILE), jnp.bfloat16),
            pltpu.VMEM((members, 2 * ROWS, TILE), jnp.bfloat16),
            pltpu.VMEM((members + ROWS, ROWS, TILE), jnp.float32),
            pltpu.VMEM((members + ROWS, 2 * ROWS, 2 * TILE), jnp.float32),
            pltpu.VMEM((members + 1, ROWS, 2 * TILE), jnp.float32),
            pltpu.VMEM((members, ROWS, TILE), jnp.float32),
            pltpu.VMEM((2, windows, ROWS, TILE), jnp.float32),
            pltpu.VMEM((2, ROWS, TILE), jnp.float32),
            pltpu.VMEM((members, ROWS, TILE), jnp.float32),
            pltpu.SemaphoreType.DMA((9,)),
            pltpu.SemaphoreType.DMA,
            pltpu.SemaphoreType.DMA((4,)),
            pltpu.SemaphoreType.DMA,
            pltpu.SemaphoreType.DMA((2,)),
            pltpu.SemaphoreType.DMA,
            pltpu.SemaphoreType.DMA,
        ],
        compiler_params=pltpu.CompilerParams(
            collective_id=0, has_side_effects=True, vmem_limit_bytes=60 * 1024 * 1024
        ),
    )(*[pltpu.with_memory_space_constraint(array, pltpu.HBM) for array in (*arrays, *tables)])


def solution(mesh):
    members, windows = mesh.shape["ctx"], mesh.shape["dp"]
    tables = transform_tables()

    def run(*arrays):
        return per_device(members, windows, [jnp.asarray(table) for table in tables], *arrays)

    return jax.shard_map(
        run,
        mesh=mesh,
        in_specs=(P("dp", "ctx", None),) * 4 + (P("dp", None),),
        out_specs=P("ctx", None),
        check_vma=False,
    )
```

```python
import functools

import jax
import jax.numpy as jnp
import numpy as np
from jax import lax
from jax.experimental import pallas as pl
from jax.experimental.pallas import tpu as pltpu
from jax.sharding import PartitionSpec as P

TILE = 128
ROWS = 8
MESH = pl.DeviceIdType.MESH


def transform_tables():
    positions = np.arange(TILE)
    theta = 2.0 * np.pi * (np.arange(TILE) + 0.5) / (2 * TILE)
    forward = np.concatenate(
        [np.cos(positions[:, None] * theta), -np.sin(positions[:, None] * theta)], axis=1
    )
    inverse = np.concatenate(
        [np.cos(theta[:, None] * positions), -np.sin(theta[:, None] * positions)], axis=0
    )
    inverse = inverse / TILE
    split = []
    for table in (forward, inverse):
        table = table.astype(np.float32)
        high = table.astype(jnp.bfloat16)
        split += [high, (table - high.astype(np.float32)).astype(jnp.bfloat16)]
    return split


def product(left, right):
    return jnp.dot(left, right, preferred_element_type=jnp.float32)


def wrap(index, size):
    return lax.rem(index + 8 * size, size)


PLAN = [
    [
        [[7, 6, 2, 4, 5, 1, 0, 3], [5, 2, 4, 3, 1, 6, 7, 0], [3, 0, 4, 5, 6, 2, 1, 7], [1, 2, 5, 6, 0, 7, 3, 4]],
        [[1, 7, 5, 0, 4, 3, 6, 2], [2, 1, 0, 5, 4, 6, 3, 7], [3, 5, 7, 1, 0, 4, 6, 2], [7, 5, 4, 3, 0, 2, 1, 6]],
        [[4, 2, 3, 0, 6, 7, 5, 1], [7, 5, 2, 6, 3, 4, 1, 0], [2, 4, 0, 1, 6, 5, 7, 3], [4, 7, 2, 6, 1, 0, 3, 5]],
        [[3, 6, 7, 5, 1, 0, 4, 2], [5, 2, 3, 1, 7, 6, 0, 4], [5, 0, 4, 2, 3, 1, 6, 7], [0, 3, 1, 4, 7, 2, 5, 6]],
        [[4, 3, 1, 2, 5, 7, 6, 0], [0, 1, 6, 7, 2, 5, 3, 4], [0, 1, 6, 7, 5, 3, 4, 2], [6, 7, 5, 4, 3, 2, 1, 0]],
        [[1, 5, 3, 2, 7, 4, 0, 6], [0, 4, 1, 5, 2, 7, 6, 3], [1, 0, 2, 7, 6, 3, 4, 5], [5, 0, 7, 3, 4, 6, 2, 1]],
        [[2, 6, 5, 3, 7, 1, 0, 4], [6, 1, 0, 4, 7, 3, 2, 5], [2, 4, 1, 6, 3, 5, 0, 7], [3, 2, 6, 7, 5, 1, 4, 0]],
        [[6, 3, 7, 2, 4, 0, 5, 1], [6, 7, 3, 0, 1, 4, 2, 5], [7, 4, 6, 1, 2, 0, 5, 3], [4, 7, 0, 1, 2, 5, 3, 6]],
    ],
    [
        [[5, 6, 4, 0, 3, 1, 7, 2], [2, 6, 0, 3, 4, 5, 1, 7], [7, 5, 3, 1, 4, 0, 2, 6], [0, 1, 7, 3, 2, 4, 6, 5]],
        [[4, 2, 6, 1, 5, 7, 0, 3], [7, 2, 6, 5, 0, 4, 3, 1], [3, 7, 0, 6, 1, 2, 5, 4], [6, 3, 2, 5, 4, 1, 0, 7]],
        [[3, 5, 1, 7, 6, 0, 4, 2], [2, 4, 5, 1, 7, 3, 6, 0], [5, 3, 4, 7, 1, 0, 6, 2], [2, 0, 1, 5, 7, 6, 3, 4]],
        [[0, 4, 7, 6, 2, 1, 3, 5], [6, 0, 1, 2, 3, 5, 7, 4], [5, 0, 1, 2, 4, 7, 6, 3], [3, 6, 4, 5, 2, 7, 1, 0]],
        [[1, 6, 2, 3, 5, 7, 4, 0], [0, 4, 7, 3, 5, 2, 1, 6], [1, 7, 2, 4, 3, 6, 5, 0], [0, 1, 7, 3, 6, 2, 4, 5]],
        [[0, 1, 6, 7, 3, 5, 4, 2], [6, 0, 5, 3, 7, 4, 2, 1], [4, 2, 5, 7, 3, 6, 0, 1], [5, 4, 3, 6, 7, 2, 1, 0]],
        [[2, 5, 1, 4, 7, 0, 3, 6], [2, 3, 0, 4, 7, 1, 6, 5], [1, 0, 3, 7, 6, 5, 2, 4], [6, 2, 4, 7, 5, 3, 0, 1]],
        [[4, 1, 5, 2, 0, 6, 7, 3], [4, 6, 2, 0, 1, 3, 5, 7], [7, 1, 0, 6, 4, 2, 5, 3], [1, 7, 3, 4, 5, 0, 2, 6]],
    ],
]


def plan_row(half, slot, core, depth, y, ring):
    return PLAN[half][y][2 * slot + core][depth] if ring == 8 else (y + depth) % ring


def select(codes, member, ring):
    code = jnp.where(member % 2 == 0, codes[0], codes[1])
    return jnp.bitwise_and(jnp.right_shift(code, 3 * (member // 2 % ring)), 7)


def depth_at(half, row, member, slot, ring):
    codes = []
    for core in range(2):
        rows = [[plan_row(half, slot, core, depth, y, ring) for depth in range(ring)] for y in range(ring)]
        codes.append(sum(rows[y].index(row) << 3 * y for y in range(ring)))
    return select(codes, member, ring)


def lag_at(half, depth, member, slot, ring):
    codes = [
        sum(plan_row(half, slot, core, depth, y, ring) << 3 * y for y in range(ring)) for core in range(2)
    ]
    return (half * ring + select(codes, member, ring)) * 2 + slot


def lag_of(window, member, slot, ring):
    mine = lax.rem(window // ring + member // (2 * ring), 2) * ring + window % ring
    lag = lag_at(0, 0, member, slot, ring)
    for place in range(1, 2 * ring):
        lag = jnp.where(mine == place, lag_at(place // ring, place % ring, member, slot, ring), lag)
    return lag


def remote(source, target, send_sem, recv_sem, **place):
    return pltpu.make_async_remote_copy(
        src_ref=source, dst_ref=target, send_sem=send_sem, recv_sem=recv_sem,
        device_id=place, device_id_type=MESH,
    )


def wait_bytes(ref, sem):
    pltpu.make_async_copy(ref, ref, sem).wait()


def kernel(
    members, windows, out_grad, gate_out, gate_in, values, doc_tiles, fwd_high, fwd_low, inv_high, inv_low, out,
    og, go, gi, va, lengths, fwd, inv,
    outgoing, incoming, docs, spectra, sums, lags, parts, total, landing,
    load_sems, tile_send, tile_recv, lag_send, lag_recv, last_send, last_recv, window_sem,
):
    me = lax.axis_index("ctx")
    window = lax.axis_index("dp")
    ring = windows // 2
    channels = members * ROWS
    my_half, my_row, my_core = me // (2 * ring), me // 2 % ring, me % 2

    def member_at(half, row, core):
        return (lax.rem(my_half + half, 2) * ring + lax.rem(my_row + row, ring)) * 2 + lax.rem(
            my_core + core, 2
        )

    gaps = [[0] + ([1, ring - 1] if ring > 2 else [1])]
    gaps += [[gap, ring - gap] for gap in range(2, ring // 2)]
    gaps += [[ring // 2]] if ring > 2 else []
    groups = [
        [(half, gap, core) for gap in group for half in (1, 0) for core in (0, 1) if half + gap + core]
        for group in gaps
    ]
    far_first = [place for group in reversed(groups) for place in reversed(group)]

    barrier = pltpu.get_barrier_semaphore()
    for place in far_first:
        pl.semaphore_signal(barrier, 1, device_id={"ctx": member_at(*place)}, device_id_type=MESH)
    early = window % ring < ring // 2
    for depth in reversed(range(ring)):
        for low in range(2):
            known = depth >= ring // 2

            @pl.when((low * ring + depth != window) & (early | known))
            def _():
                pl.semaphore_signal(barrier, 1, device_id={"dp": low * ring + depth}, device_id_type=MESH)

    pairs = [
        (out_grad, og), (gate_out, go), (gate_in, gi), (values, va), (doc_tiles, lengths),
        (fwd_high, fwd.at[pl.ds(0, TILE)]), (fwd_low, fwd.at[pl.ds(TILE, TILE)]),
        (inv_high, inv.at[0]), (inv_low, inv.at[1]),
    ]
    loads = [
        pltpu.make_async_copy(source, target, load_sems.at[n]) for n, (source, target) in enumerate(pairs)
    ]
    for load in loads:
        load.start()
    for load in loads:
        load.wait()

    weighted = go[0].astype(jnp.float32) * og[0].astype(jnp.float32)
    gated = gi[0].astype(jnp.float32) * va[0].astype(jnp.float32)
    weighted = weighted.T.reshape(members, 1, ROWS, TILE)
    gated = gated.T.reshape(members, 1, ROWS, TILE)
    outgoing[...] = (
        jnp.concatenate([weighted, gated], axis=1)
        .reshape(members, 2 * ROWS, TILE)
        .astype(jnp.bfloat16)
    )
    incoming[me] = outgoing[me]

    tile = lax.broadcasted_iota(jnp.int32, docs.shape, 0)
    label = jnp.zeros(docs.shape, jnp.float32)
    end = jnp.int32(0)
    for entry in range(lengths.shape[1]):
        end = end + lengths[0, entry]
        label += (tile >= end).astype(jnp.float32)
    docs[...] = label
    spectra[pl.ds(members, ROWS)] = jnp.zeros((ROWS, 2 * ROWS, 2 * TILE), jnp.float32)
    sums[members] = jnp.zeros((ROWS, 2 * TILE), jnp.float32)

    pl.semaphore_wait(barrier, members - 1 + jnp.where(early, ring - 1, windows - 1))

    late_rows = sorted(range(ring), key=lambda row: min(row, ring - row), reverse=True)
    late_first = [(row, half, core) for row in late_rows for half in range(2) for core in range(2)]
    for row, half, core in late_first:
        peer = (half * ring + row) * 2 + core
        gap = wrap(row - my_row, ring)
        number = jnp.maximum(jnp.minimum(gap, ring - gap) - 1, 0)

        @pl.when(peer != me)
        def _():
            remote(
                outgoing.at[peer], incoming.at[me], tile_send, tile_recv.at[number], ctx=peer
            ).start()

    @pl.when(jnp.logical_not(early))
    def _():
        for depth in range(ring // 2):
            for low in range(2):
                pl.semaphore_signal(window_sem, 1, device_id={"dp": low * ring + depth}, device_id_type=MESH)

    for number, group in enumerate(groups):
        wait_bytes(incoming.at[pl.ds(0, len(group))], tile_recv.at[number])
        places = sorted({(half, gap) for half, gap, _ in group})
        if number == 0:
            places = sorted(set(places) | {(0, 0)})
        starts = [
            (lax.rem(my_half + half, 2) * ring + lax.rem(my_row + gap, ring)) * 2 for half, gap in places
        ]
        tiles = jnp.concatenate(
            [incoming[pl.ds(start, 2)].reshape(4 * ROWS, TILE) for start in starts], axis=0
        )
        hats = product(jnp.concatenate([tiles, tiles], axis=1), fwd[...])
        for number_, start in enumerate(starts):
            spectra[pl.ds(start, 2)] = hats[number_ * 4 * ROWS : (number_ + 1) * 4 * ROWS].reshape(
                2, 2 * ROWS, 2 * TILE
            )

    def add_pairs(first, stop, terms):
        def lag_block(lag, carried):
            real = jnp.zeros((ROWS, TILE), jnp.float32)
            imag = jnp.zeros((ROWS, TILE), jnp.float32)
            for source in range(terms):
                head = source + lag
                head_real = spectra[head, :ROWS, :TILE]
                head_imag = spectra[head, :ROWS, TILE:]
                tail_real = spectra[source, ROWS:, :TILE]
                tail_imag = spectra[source, ROWS:, TILE:]
                same = docs[head] == docs[source]
                real += jnp.where(same, head_real * tail_real + head_imag * tail_imag, 0.0)
                imag += jnp.where(same, head_imag * tail_real - head_real * tail_imag, 0.0)
            sums[lag, :, :TILE] = real
            sums[lag, :, TILE:] = imag
            return carried

        lax.fori_loop(first, stop, lag_block, 0)

    quarter = members // 4
    parity = lax.broadcasted_iota(jnp.int32, (quarter * ROWS, TILE), 1) % 2
    sign = (1 - 2 * parity).astype(jnp.float32)

    def back_and_send(first):
        here = sums[pl.ds(first, quarter)].reshape(quarter * ROWS, 2 * TILE)
        after = sums[pl.ds(first + 1, quarter)].reshape(quarter * ROWS, 2 * TILE)
        both = jnp.concatenate(
            [here[:, :TILE] + sign * after[:, TILE:], here[:, TILE:] - sign * after[:, :TILE]], axis=1
        )
        high = both.astype(jnp.bfloat16)
        low = (both - high.astype(jnp.float32)).astype(jnp.bfloat16)
        result = product(high, inv[0]) + product(low, inv[0]) + product(high, inv[1])
        lags[pl.ds(first, quarter)] = result.reshape(quarter, ROWS, TILE)
        half = first // (2 * ring)
        base = lax.rem(half + my_half, 2) * ring
        for lag in range(first, first + quarter):
            slot = lag % 2
            owner = base + depth_at(half, lag // 2 % ring, me, slot, ring)

            @pl.when(owner != window)
            def _():
                remote(
                    lags.at[lag], parts.at[slot, window], lag_send, lag_recv.at[slot], dp=owner
                ).start()

    add_pairs(0, quarter + 1, members)

    @pl.when(early)
    def _():
        pl.semaphore_wait(window_sem, ring)

    back_and_send(0)
    add_pairs(quarter + 1, 2 * quarter + 1, members - quarter)
    back_and_send(quarter)
    add_pairs(2 * quarter + 1, 3 * quarter + 1, 2 * quarter)
    back_and_send(2 * quarter)
    add_pairs(3 * quarter + 1, members, quarter)
    back_and_send(3 * quarter)

    mine = [lag_of(window, me, slot, ring) for slot in range(2)]
    for slot in range(2):
        parts[slot, window] = lags[mine[slot]]
    lead = (mine[1] // 2 <= mine[0] // 2).astype(jnp.int32)

    def spread(slot, depths):
        lag = jnp.where(slot == 0, mine[0], mine[1])
        for depth in depths:
            for low in range(2):
                reader = low * ring + depth
                own = (reader == window) & (lag == me)

                @pl.when(own)
                def _():
                    pltpu.make_async_copy(total.at[slot], landing.at[me], last_recv).start()

                @pl.when(jnp.logical_not(own))
                def _():
                    remote(
                        total.at[slot], landing.at[me], last_send, last_recv, ctx=lag, dp=reader
                    ).start()

    for slot in (lead, 1 - lead):
        wait_bytes(parts.at[slot, pl.ds(0, windows - 1)], lag_recv.at[slot])
        total[slot] = jnp.sum(parts[slot], axis=0)
        spread(slot, range(2))
    for depth in range(2, ring):
        spread(lead, [depth])
        spread(1 - lead, [depth])

    wait_bytes(landing, last_recv)
    out[...] = landing[...].reshape(channels, TILE).T

    wait_bytes(outgoing.at[pl.ds(0, members - 1)], tile_send)
    wait_bytes(lags.at[pl.ds(0, members - 2)], lag_send)
    keeps = (mine[0] == me) | (mine[1] == me)

    @pl.when(keeps)
    def _():
        wait_bytes(landing.at[pl.ds(0, members - 1)], last_send)

    @pl.when(jnp.logical_not(keeps))
    def _():
        wait_bytes(landing, last_send)


def per_device(members, windows, tables, *arrays):
    channels = members * ROWS
    hbm = pl.BlockSpec(memory_space=pltpu.HBM)
    return pl.pallas_call(
        functools.partial(kernel, members, windows),
        out_shape=pltpu.VMEM((TILE, channels), jnp.float32),
        in_specs=[hbm] * 9,
        out_specs=pl.BlockSpec(memory_space=pltpu.VMEM),
        scratch_shapes=[
            pltpu.VMEM((1, TILE, channels), jnp.bfloat16),
            pltpu.VMEM((1, TILE, channels), jnp.bfloat16),
            pltpu.VMEM((1, TILE, channels), jnp.bfloat16),
            pltpu.VMEM((1, TILE, channels), jnp.bfloat16),
            pltpu.SMEM(arrays[4].shape, jnp.int32),
            pltpu.VMEM((2 * TILE, 2 * TILE), jnp.bfloat16),
            pltpu.VMEM((2, 2 * TILE, TILE), jnp.bfloat16),
            pltpu.VMEM((members, 2 * ROWS, TILE), jnp.bfloat16),
            pltpu.VMEM((members, 2 * ROWS, TILE), jnp.bfloat16),
            pltpu.VMEM((members + ROWS, ROWS, TILE), jnp.float32),
            pltpu.VMEM((members + ROWS, 2 * ROWS, 2 * TILE), jnp.float32),
            pltpu.VMEM((members + 1, ROWS, 2 * TILE), jnp.float32),
            pltpu.VMEM((members, ROWS, TILE), jnp.float32),
            pltpu.VMEM((2, windows, ROWS, TILE), jnp.float32),
            pltpu.VMEM((2, ROWS, TILE), jnp.float32),
            pltpu.VMEM((members, ROWS, TILE), jnp.float32),
            pltpu.SemaphoreType.DMA((9,)),
            pltpu.SemaphoreType.DMA,
            pltpu.SemaphoreType.DMA((4,)),
            pltpu.SemaphoreType.DMA,
            pltpu.SemaphoreType.DMA((2,)),
            pltpu.SemaphoreType.DMA,
            pltpu.SemaphoreType.DMA,
            pltpu.SemaphoreType.REGULAR,
        ],
        compiler_params=pltpu.CompilerParams(
            collective_id=0, has_side_effects=True, vmem_limit_bytes=60 * 1024 * 1024
        ),
    )(*[pltpu.with_memory_space_constraint(array, pltpu.HBM) for array in (*arrays, *tables)])


def solution(mesh):
    members, windows = mesh.shape["ctx"], mesh.shape["dp"]
    tables = transform_tables()

    def run(*arrays):
        return per_device(members, windows, [jnp.asarray(table) for table in tables], *arrays)

    return jax.shard_map(
        run,
        mesh=mesh,
        in_specs=(P("dp", "ctx", None),) * 4 + (P("dp", None),),
        out_specs=P("ctx", None),
        check_vma=False,
    )
```

```python
import functools

import jax
import jax.numpy as jnp
import numpy as np
from jax import lax
from jax.experimental import pallas as pl
from jax.experimental.pallas import tpu as pltpu
from jax.sharding import PartitionSpec as P

TILE = 128
ROWS = 8
MESH = pl.DeviceIdType.MESH


def transform_tables():
    positions = np.arange(TILE)
    theta = 2.0 * np.pi * (np.arange(TILE) + 0.5) / (2 * TILE)
    forward = np.concatenate(
        [np.cos(positions[:, None] * theta), -np.sin(positions[:, None] * theta)], axis=1
    )
    inverse = np.concatenate(
        [np.cos(theta[:, None] * positions), -np.sin(theta[:, None] * positions)], axis=0
    )
    inverse = inverse / TILE
    split = []
    for table in (forward, inverse):
        table = table.astype(np.float32)
        high = table.astype(jnp.bfloat16)
        split += [high, (table - high.astype(np.float32)).astype(jnp.bfloat16)]
    return split


def product(left, right):
    return jnp.dot(left, right, preferred_element_type=jnp.float32)


def wrap(index, size):
    return lax.rem(index + 8 * size, size)


PLAN = [
    [
        [[2, 6, 5, 0, 4, 3, 1, 7], [4, 6, 2, 0, 7, 5, 1, 3], [7, 4, 0, 3, 1, 5, 6, 2], [3, 0, 6, 1, 2, 4, 7, 5]],
        [[6, 2, 0, 5, 1, 7, 4, 3], [7, 3, 0, 6, 5, 2, 4, 1], [0, 7, 3, 1, 5, 4, 2, 6], [2, 3, 1, 5, 4, 0, 7, 6]],
        [[3, 2, 4, 5, 7, 0, 6, 1], [1, 0, 4, 7, 6, 2, 5, 3], [5, 4, 7, 3, 1, 6, 0, 2], [6, 0, 2, 7, 3, 5, 1, 4]],
        [[3, 0, 4, 1, 7, 6, 2, 5], [2, 6, 7, 5, 1, 3, 0, 4], [5, 3, 1, 4, 2, 7, 0, 6], [6, 4, 7, 2, 5, 1, 3, 0]],
        [[3, 0, 5, 6, 2, 4, 7, 1], [0, 6, 7, 4, 3, 1, 2, 5], [1, 4, 6, 2, 3, 7, 5, 0], [4, 7, 1, 2, 6, 3, 5, 0]],
        [[1, 5, 2, 6, 7, 3, 4, 0], [1, 2, 6, 3, 7, 5, 0, 4], [0, 1, 3, 7, 4, 2, 6, 5], [4, 2, 5, 7, 3, 6, 0, 1]],
        [[2, 5, 1, 7, 4, 0, 3, 6], [5, 4, 0, 3, 7, 6, 1, 2], [4, 0, 5, 7, 6, 1, 2, 3], [0, 1, 4, 6, 5, 2, 3, 7]],
        [[7, 5, 6, 2, 1, 4, 3, 0], [5, 7, 3, 2, 1, 0, 6, 4], [6, 1, 3, 4, 5, 7, 0, 2], [0, 3, 2, 4, 6, 1, 5, 7]],
    ],
    [
        [[5, 6, 0, 2, 1, 3, 4, 7], [1, 5, 6, 3, 2, 4, 0, 7], [2, 0, 3, 7, 4, 5, 1, 6], [7, 2, 1, 6, 4, 0, 5, 3]],
        [[5, 1, 4, 7, 3, 6, 2, 0], [3, 0, 5, 4, 7, 6, 2, 1], [1, 5, 2, 6, 7, 0, 4, 3], [7, 3, 5, 4, 2, 0, 1, 6]],
        [[2, 3, 0, 7, 1, 4, 6, 5], [5, 0, 3, 1, 7, 2, 6, 4], [0, 2, 7, 5, 4, 6, 3, 1], [3, 4, 6, 2, 5, 1, 7, 0]],
        [[4, 7, 6, 2, 5, 3, 0, 1], [7, 4, 1, 6, 2, 5, 0, 3], [4, 0, 7, 2, 3, 1, 5, 6], [0, 7, 1, 3, 2, 6, 4, 5]],
        [[6, 4, 7, 2, 5, 1, 0, 3], [5, 6, 3, 7, 2, 1, 4, 0], [0, 1, 4, 5, 3, 7, 6, 2], [1, 5, 2, 3, 6, 7, 4, 0]],
        [[5, 3, 2, 7, 6, 4, 0, 1], [0, 1, 6, 5, 7, 2, 3, 4], [1, 0, 4, 7, 3, 6, 2, 5], [2, 1, 4, 3, 7, 5, 6, 0]],
        [[4, 6, 0, 3, 7, 1, 5, 2], [6, 1, 0, 4, 3, 2, 7, 5], [0, 6, 3, 4, 7, 5, 2, 1], [1, 3, 5, 7, 4, 6, 0, 2]],
        [[2, 5, 1, 6, 7, 0, 3, 4], [4, 2, 0, 5, 6, 3, 1, 7], [3, 0, 5, 7, 6, 2, 1, 4], [6, 3, 1, 7, 5, 0, 4, 2]],
    ],
]


def plan_row(half, slot, core, depth, y, ring):
    return PLAN[half][y][2 * slot + core][depth] if ring == 8 else (y + depth) % ring


def select(codes, member, ring):
    code = jnp.where(member % 2 == 0, codes[0], codes[1])
    return jnp.bitwise_and(jnp.right_shift(code, 3 * (member // 2 % ring)), 7)


def depth_at(half, row, member, slot, ring):
    codes = []
    for core in range(2):
        rows = [[plan_row(half, slot, core, depth, y, ring) for depth in range(ring)] for y in range(ring)]
        codes.append(sum(rows[y].index(row) << 3 * y for y in range(ring)))
    return select(codes, member, ring)


def lag_at(half, depth, member, slot, ring):
    codes = [
        sum(plan_row(half, slot, core, depth, y, ring) << 3 * y for y in range(ring)) for core in range(2)
    ]
    return (half * ring + select(codes, member, ring)) * 2 + slot


def lag_of(window, member, slot, ring):
    mine = lax.rem(window // ring + member // (2 * ring), 2) * ring + window % ring
    lag = lag_at(0, 0, member, slot, ring)
    for place in range(1, 2 * ring):
        lag = jnp.where(mine == place, lag_at(place // ring, place % ring, member, slot, ring), lag)
    return lag


def remote(source, target, send_sem, recv_sem, **place):
    return pltpu.make_async_remote_copy(
        src_ref=source, dst_ref=target, send_sem=send_sem, recv_sem=recv_sem,
        device_id=place, device_id_type=MESH,
    )


def wait_bytes(ref, sem):
    pltpu.make_async_copy(ref, ref, sem).wait()


def kernel(
    members, windows, out_grad, gate_out, gate_in, values, doc_tiles, fwd_high, fwd_low, inv_high, inv_low, out,
    og, go, gi, va, lengths, fwd, inv,
    outgoing, incoming, docs, spectra, sums, lags, parts, total, landing,
    load_sems, tile_send, tile_recv, lag_send, lag_recv, last_send, last_recv, window_sem,
):
    me = lax.axis_index("ctx")
    window = lax.axis_index("dp")
    ring = windows // 2
    channels = members * ROWS
    my_half, my_row, my_core = me // (2 * ring), me // 2 % ring, me % 2

    def member_at(half, row, core):
        return (lax.rem(my_half + half, 2) * ring + lax.rem(my_row + row, ring)) * 2 + lax.rem(
            my_core + core, 2
        )

    gaps = [[0] + ([1, ring - 1] if ring > 2 else [1])]
    gaps += [[gap, ring - gap] for gap in range(2, ring // 2)]
    gaps += [[ring // 2]] if ring > 2 else []
    groups = [
        [(half, gap, core) for gap in group for half in (1, 0) for core in (0, 1) if half + gap + core]
        for group in gaps
    ]
    far_first = [place for group in reversed(groups) for place in reversed(group)]

    barrier = pltpu.get_barrier_semaphore()
    for place in far_first:
        pl.semaphore_signal(barrier, 1, device_id={"ctx": member_at(*place)}, device_id_type=MESH)
    early = window % ring < ring // 2
    for depth in reversed(range(ring)):
        for low in range(2):
            known = depth >= ring // 2

            @pl.when((low * ring + depth != window) & (early | known))
            def _():
                pl.semaphore_signal(barrier, 1, device_id={"dp": low * ring + depth}, device_id_type=MESH)

    pairs = [
        (out_grad, og), (gate_out, go), (gate_in, gi), (values, va), (doc_tiles, lengths),
        (fwd_high, fwd.at[pl.ds(0, TILE)]), (fwd_low, fwd.at[pl.ds(TILE, TILE)]),
        (inv_high, inv.at[0]), (inv_low, inv.at[1]),
    ]
    loads = [
        pltpu.make_async_copy(source, target, load_sems.at[n]) for n, (source, target) in enumerate(pairs)
    ]
    for load in loads:
        load.start()
    for load in loads:
        load.wait()

    weighted = go[0].astype(jnp.float32) * og[0].astype(jnp.float32)
    gated = gi[0].astype(jnp.float32) * va[0].astype(jnp.float32)
    weighted = weighted.T.reshape(members, 1, ROWS, TILE)
    gated = gated.T.reshape(members, 1, ROWS, TILE)
    outgoing[...] = (
        jnp.concatenate([weighted, gated], axis=1)
        .reshape(members, 2 * ROWS, TILE)
        .astype(jnp.bfloat16)
    )
    incoming[me] = outgoing[me]

    tile = lax.broadcasted_iota(jnp.int32, docs.shape, 0)
    label = jnp.zeros(docs.shape, jnp.float32)
    end = jnp.int32(0)
    for entry in range(lengths.shape[1]):
        end = end + lengths[0, entry]
        label += (tile >= end).astype(jnp.float32)
    docs[...] = label
    spectra[pl.ds(members, ROWS)] = jnp.zeros((ROWS, 2 * ROWS, 2 * TILE), jnp.float32)
    sums[members] = jnp.zeros((ROWS, 2 * TILE), jnp.float32)

    pl.semaphore_wait(barrier, members - 1 + jnp.where(early, ring - 1, windows - 1))


    mixed_rows = [row % ring for row in (4, 1, 3, 7, 5, 2, 6, 0)][-ring:]
    mixed_rows = sorted(set(mixed_rows), key=mixed_rows.index)
    mixed = [(row, half, core) for core in range(2) for half in (1, 0) for row in mixed_rows]
    for row_step, half_step, core_step in mixed:
        if row_step + half_step + core_step == 0:
            continue
        row = lax.rem(my_row + row_step, ring)
        peer = (lax.rem(my_half + half_step, 2) * ring + row) * 2 + lax.rem(my_core + core_step, 2)
        gap = wrap(row - my_row, ring)
        number = jnp.maximum(jnp.minimum(gap, ring - gap) - 1, 0)

        remote(
            outgoing.at[peer], incoming.at[me], tile_send, tile_recv.at[number], ctx=peer
        ).start()

    @pl.when(jnp.logical_not(early))
    def _():
        for depth in range(ring // 2):
            for low in range(2):
                pl.semaphore_signal(window_sem, 1, device_id={"dp": low * ring + depth}, device_id_type=MESH)

    for number, group in enumerate(groups):
        wait_bytes(incoming.at[pl.ds(0, len(group))], tile_recv.at[number])
        places = sorted({(half, gap) for half, gap, _ in group})
        if number == 0:
            places = sorted(set(places) | {(0, 0)})
        starts = [
            (lax.rem(my_half + half, 2) * ring + lax.rem(my_row + gap, ring)) * 2 for half, gap in places
        ]
        tiles = jnp.concatenate(
            [incoming[pl.ds(start, 2)].reshape(4 * ROWS, TILE) for start in starts], axis=0
        )
        hats = product(jnp.concatenate([tiles, tiles], axis=1), fwd[...])
        for number_, start in enumerate(starts):
            spectra[pl.ds(start, 2)] = hats[number_ * 4 * ROWS : (number_ + 1) * 4 * ROWS].reshape(
                2, 2 * ROWS, 2 * TILE
            )

    def add_pairs(first, stop, terms):
        def lag_block(lag, carried):
            real = jnp.zeros((ROWS, TILE), jnp.float32)
            imag = jnp.zeros((ROWS, TILE), jnp.float32)
            for source in range(terms):
                head = source + lag
                head_real = spectra[head, :ROWS, :TILE]
                head_imag = spectra[head, :ROWS, TILE:]
                tail_real = spectra[source, ROWS:, :TILE]
                tail_imag = spectra[source, ROWS:, TILE:]
                same = docs[head] == docs[source]
                real += jnp.where(same, head_real * tail_real + head_imag * tail_imag, 0.0)
                imag += jnp.where(same, head_imag * tail_real - head_real * tail_imag, 0.0)
            sums[lag, :, :TILE] = real
            sums[lag, :, TILE:] = imag
            return carried

        lax.fori_loop(first, stop, lag_block, 0)

    quarter = members // 4
    parity = lax.broadcasted_iota(jnp.int32, (quarter * ROWS, TILE), 1) % 2
    sign = (1 - 2 * parity).astype(jnp.float32)

    def back_and_send(first):
        here = sums[pl.ds(first, quarter)].reshape(quarter * ROWS, 2 * TILE)
        after = sums[pl.ds(first + 1, quarter)].reshape(quarter * ROWS, 2 * TILE)
        both = jnp.concatenate(
            [here[:, :TILE] + sign * after[:, TILE:], here[:, TILE:] - sign * after[:, :TILE]], axis=1
        )
        high = both.astype(jnp.bfloat16)
        low = (both - high.astype(jnp.float32)).astype(jnp.bfloat16)
        result = product(high, inv[0]) + product(low, inv[0]) + product(high, inv[1])
        lags[pl.ds(first, quarter)] = result.reshape(quarter, ROWS, TILE)
        half = first // (2 * ring)
        base = lax.rem(half + my_half, 2) * ring
        for lag in range(first, first + quarter):
            slot = lag % 2
            owner = base + depth_at(half, lag // 2 % ring, me, slot, ring)

            @pl.when(owner != window)
            def _():
                remote(
                    lags.at[lag], parts.at[slot, window], lag_send, lag_recv.at[slot], dp=owner
                ).start()

    add_pairs(0, quarter + 1, members)

    @pl.when(early)
    def _():
        pl.semaphore_wait(window_sem, ring)

    back_and_send(0)
    add_pairs(quarter + 1, 2 * quarter + 1, members - quarter)
    back_and_send(quarter)
    add_pairs(2 * quarter + 1, 3 * quarter + 1, 2 * quarter)
    back_and_send(2 * quarter)
    add_pairs(3 * quarter + 1, members, quarter)
    back_and_send(3 * quarter)

    mine = [lag_of(window, me, slot, ring) for slot in range(2)]
    for slot in range(2):
        parts[slot, window] = lags[mine[slot]]
    lead = (mine[1] // 2 <= mine[0] // 2).astype(jnp.int32)

    def spread(slot, depths):
        lag = jnp.where(slot == 0, mine[0], mine[1])
        for depth in depths:
            for low in range(2):
                reader = low * ring + depth
                own = (reader == window) & (lag == me)

                @pl.when(own)
                def _():
                    pltpu.make_async_copy(total.at[slot], landing.at[me], last_recv).start()

                @pl.when(jnp.logical_not(own))
                def _():
                    remote(
                        total.at[slot], landing.at[me], last_send, last_recv, ctx=lag, dp=reader
                    ).start()

    for slot in (lead, 1 - lead):
        wait_bytes(parts.at[slot, pl.ds(0, windows - 1)], lag_recv.at[slot])
        total[slot] = jnp.sum(parts[slot], axis=0)
        spread(slot, range(2))
    for depth in range(2, ring):
        spread(lead, [depth])
        spread(1 - lead, [depth])

    wait_bytes(landing, last_recv)
    out[...] = landing[...].reshape(channels, TILE).T

    wait_bytes(outgoing.at[pl.ds(0, members - 1)], tile_send)
    wait_bytes(lags.at[pl.ds(0, members - 2)], lag_send)
    keeps = (mine[0] == me) | (mine[1] == me)

    @pl.when(keeps)
    def _():
        wait_bytes(landing.at[pl.ds(0, members - 1)], last_send)

    @pl.when(jnp.logical_not(keeps))
    def _():
        wait_bytes(landing, last_send)


def per_device(members, windows, tables, *arrays):
    channels = members * ROWS
    hbm = pl.BlockSpec(memory_space=pltpu.HBM)
    return pl.pallas_call(
        functools.partial(kernel, members, windows),
        out_shape=pltpu.VMEM((TILE, channels), jnp.float32),
        in_specs=[hbm] * 9,
        out_specs=pl.BlockSpec(memory_space=pltpu.VMEM),
        scratch_shapes=[
            pltpu.VMEM((1, TILE, channels), jnp.bfloat16),
            pltpu.VMEM((1, TILE, channels), jnp.bfloat16),
            pltpu.VMEM((1, TILE, channels), jnp.bfloat16),
            pltpu.VMEM((1, TILE, channels), jnp.bfloat16),
            pltpu.SMEM(arrays[4].shape, jnp.int32),
            pltpu.VMEM((2 * TILE, 2 * TILE), jnp.bfloat16),
            pltpu.VMEM((2, 2 * TILE, TILE), jnp.bfloat16),
            pltpu.VMEM((members, 2 * ROWS, TILE), jnp.bfloat16),
            pltpu.VMEM((members, 2 * ROWS, TILE), jnp.bfloat16),
            pltpu.VMEM((members + ROWS, ROWS, TILE), jnp.float32),
            pltpu.VMEM((members + ROWS, 2 * ROWS, 2 * TILE), jnp.float32),
            pltpu.VMEM((members + 1, ROWS, 2 * TILE), jnp.float32),
            pltpu.VMEM((members, ROWS, TILE), jnp.float32),
            pltpu.VMEM((2, windows, ROWS, TILE), jnp.float32),
            pltpu.VMEM((2, ROWS, TILE), jnp.float32),
            pltpu.VMEM((members, ROWS, TILE), jnp.float32),
            pltpu.SemaphoreType.DMA((9,)),
            pltpu.SemaphoreType.DMA,
            pltpu.SemaphoreType.DMA((4,)),
            pltpu.SemaphoreType.DMA,
            pltpu.SemaphoreType.DMA((2,)),
            pltpu.SemaphoreType.DMA,
            pltpu.SemaphoreType.DMA,
            pltpu.SemaphoreType.REGULAR,
        ],
        compiler_params=pltpu.CompilerParams(
            collective_id=0, has_side_effects=True, vmem_limit_bytes=60 * 1024 * 1024
        ),
    )(*[pltpu.with_memory_space_constraint(array, pltpu.HBM) for array in (*arrays, *tables)])


def solution(mesh):
    members, windows = mesh.shape["ctx"], mesh.shape["dp"]
    tables = transform_tables()

    def run(*arrays):
        return per_device(members, windows, [jnp.asarray(table) for table in tables], *arrays)

    return jax.shard_map(
        run,
        mesh=mesh,
        in_specs=(P("dp", "ctx", None),) * 4 + (P("dp", None),),
        out_specs=P("ctx", None),
        check_vma=False,
    )
```

```python
import functools

import jax
import jax.numpy as jnp
import numpy as np
from jax import lax
from jax.experimental import pallas as pl
from jax.experimental.pallas import tpu as pltpu
from jax.sharding import PartitionSpec as P

TILE = 128
ROWS = 8
MESH = pl.DeviceIdType.MESH


def transform_tables():
    positions = np.arange(TILE)
    theta = 2.0 * np.pi * (np.arange(TILE) + 0.5) / (2 * TILE)
    forward = np.concatenate(
        [np.cos(positions[:, None] * theta), -np.sin(positions[:, None] * theta)], axis=1
    )
    inverse = np.concatenate(
        [np.cos(theta[:, None] * positions), -np.sin(theta[:, None] * positions)], axis=0
    )
    inverse = inverse / TILE
    split = []
    for table in (forward, inverse):
        table = table.astype(np.float32)
        high = table.astype(jnp.bfloat16)
        split += [high, (table - high.astype(np.float32)).astype(jnp.bfloat16)]
    return split


def product(left, right):
    return jnp.dot(left, right, preferred_element_type=jnp.float32)


def wrap(index, size):
    return lax.rem(index + 8 * size, size)


PLAN = [
    [
        [[2, 6, 5, 0, 4, 3, 1, 7], [4, 6, 2, 0, 7, 5, 1, 3], [7, 4, 0, 3, 1, 5, 6, 2], [3, 0, 6, 1, 2, 4, 7, 5]],
        [[6, 2, 0, 5, 1, 7, 4, 3], [7, 3, 0, 6, 5, 2, 4, 1], [0, 7, 3, 1, 5, 4, 2, 6], [2, 3, 1, 5, 4, 0, 7, 6]],
        [[3, 2, 4, 5, 7, 0, 6, 1], [1, 0, 4, 7, 6, 2, 5, 3], [5, 4, 7, 3, 1, 6, 0, 2], [6, 0, 2, 7, 3, 5, 1, 4]],
        [[3, 0, 4, 1, 7, 6, 2, 5], [2, 6, 7, 5, 1, 3, 0, 4], [5, 3, 1, 4, 2, 7, 0, 6], [6, 4, 7, 2, 5, 1, 3, 0]],
        [[3, 0, 5, 6, 2, 4, 7, 1], [0, 6, 7, 4, 3, 1, 2, 5], [1, 4, 6, 2, 3, 7, 5, 0], [4, 7, 1, 2, 6, 3, 5, 0]],
        [[1, 5, 2, 6, 7, 3, 4, 0], [1, 2, 6, 3, 7, 5, 0, 4], [0, 1, 3, 7, 4, 2, 6, 5], [4, 2, 5, 7, 3, 6, 0, 1]],
        [[2, 5, 1, 7, 4, 0, 3, 6], [5, 4, 0, 3, 7, 6, 1, 2], [4, 0, 5, 7, 6, 1, 2, 3], [0, 1, 4, 6, 5, 2, 3, 7]],
        [[7, 5, 6, 2, 1, 4, 3, 0], [5, 7, 3, 2, 1, 0, 6, 4], [6, 1, 3, 4, 5, 7, 0, 2], [0, 3, 2, 4, 6, 1, 5, 7]],
    ],
    [
        [[5, 6, 0, 2, 1, 3, 4, 7], [1, 5, 6, 3, 2, 4, 0, 7], [2, 0, 3, 7, 4, 5, 1, 6], [7, 2, 1, 6, 4, 0, 5, 3]],
        [[5, 1, 4, 7, 3, 6, 2, 0], [3, 0, 5, 4, 7, 6, 2, 1], [1, 5, 2, 6, 7, 0, 4, 3], [7, 3, 5, 4, 2, 0, 1, 6]],
        [[2, 3, 0, 7, 1, 4, 6, 5], [5, 0, 3, 1, 7, 2, 6, 4], [0, 2, 7, 5, 4, 6, 3, 1], [3, 4, 6, 2, 5, 1, 7, 0]],
        [[4, 7, 6, 2, 5, 3, 0, 1], [7, 4, 1, 6, 2, 5, 0, 3], [4, 0, 7, 2, 3, 1, 5, 6], [0, 7, 1, 3, 2, 6, 4, 5]],
        [[6, 4, 7, 2, 5, 1, 0, 3], [5, 6, 3, 7, 2, 1, 4, 0], [0, 1, 4, 5, 3, 7, 6, 2], [1, 5, 2, 3, 6, 7, 4, 0]],
        [[5, 3, 2, 7, 6, 4, 0, 1], [0, 1, 6, 5, 7, 2, 3, 4], [1, 0, 4, 7, 3, 6, 2, 5], [2, 1, 4, 3, 7, 5, 6, 0]],
        [[4, 6, 0, 3, 7, 1, 5, 2], [6, 1, 0, 4, 3, 2, 7, 5], [0, 6, 3, 4, 7, 5, 2, 1], [1, 3, 5, 7, 4, 6, 0, 2]],
        [[2, 5, 1, 6, 7, 0, 3, 4], [4, 2, 0, 5, 6, 3, 1, 7], [3, 0, 5, 7, 6, 2, 1, 4], [6, 3, 1, 7, 5, 0, 4, 2]],
    ],
]


def plan_row(half, slot, core, depth, y, ring):
    return PLAN[half][y][2 * slot + core][depth] if ring == 8 else (y + depth) % ring


def select(codes, member, ring):
    code = jnp.where(member % 2 == 0, codes[0], codes[1])
    return jnp.bitwise_and(jnp.right_shift(code, 3 * (member // 2 % ring)), 7)


def depth_at(half, row, member, slot, ring):
    codes = []
    for core in range(2):
        rows = [[plan_row(half, slot, core, depth, y, ring) for depth in range(ring)] for y in range(ring)]
        codes.append(sum(rows[y].index(row) << 3 * y for y in range(ring)))
    return select(codes, member, ring)


def lag_at(half, depth, member, slot, ring):
    codes = [
        sum(plan_row(half, slot, core, depth, y, ring) << 3 * y for y in range(ring)) for core in range(2)
    ]
    return (half * ring + select(codes, member, ring)) * 2 + slot


def lag_of(window, member, slot, ring):
    mine = lax.rem(window // ring + member // (2 * ring), 2) * ring + window % ring
    lag = lag_at(0, 0, member, slot, ring)
    for place in range(1, 2 * ring):
        lag = jnp.where(mine == place, lag_at(place // ring, place % ring, member, slot, ring), lag)
    return lag


def remote(source, target, send_sem, recv_sem, **place):
    return pltpu.make_async_remote_copy(
        src_ref=source, dst_ref=target, send_sem=send_sem, recv_sem=recv_sem,
        device_id=place, device_id_type=MESH,
    )


def wait_bytes(ref, sem):
    pltpu.make_async_copy(ref, ref, sem).wait()


def kernel(
    members, windows, out_grad, gate_out, gate_in, values, doc_tiles, fwd_high, fwd_low, inv_high, inv_low, out,
    og, go, gi, va, lengths, fwd, inv,
    outgoing, incoming, docs, spectra, sums, lags, parts, total, landing,
    load_sems, tile_send, tile_recv, lag_send, lag_recv, last_send, last_recv, window_sem,
):
    me = lax.axis_index("ctx")
    window = lax.axis_index("dp")
    ring = windows // 2
    channels = members * ROWS
    my_half, my_row, my_core = me // (2 * ring), me // 2 % ring, me % 2

    def member_at(half, row, core):
        return (lax.rem(my_half + half, 2) * ring + lax.rem(my_row + row, ring)) * 2 + lax.rem(
            my_core + core, 2
        )

    gaps = [[0] + ([1, ring - 1] if ring > 2 else [1])]
    gaps += [[gap, ring - gap] for gap in range(2, ring // 2)]
    gaps += [[ring // 2]] if ring > 2 else []
    groups = [
        [(half, gap, core) for gap in group for half in (1, 0) for core in (0, 1) if half + gap + core]
        for group in gaps
    ]
    far_first = [place for group in reversed(groups) for place in reversed(group)]

    barrier = pltpu.get_barrier_semaphore()
    for place in far_first:
        pl.semaphore_signal(barrier, 1, device_id={"ctx": member_at(*place)}, device_id_type=MESH)
    early = window % ring < ring // 2
    for depth in reversed(range(ring)):
        for low in range(2):
            known = depth >= ring // 2

            @pl.when((low * ring + depth != window) & (early | known))
            def _():
                pl.semaphore_signal(barrier, 1, device_id={"dp": low * ring + depth}, device_id_type=MESH)

    pairs = [
        (out_grad, og), (gate_out, go), (gate_in, gi), (values, va), (doc_tiles, lengths),
        (fwd_high, fwd.at[pl.ds(0, TILE)]), (fwd_low, fwd.at[pl.ds(TILE, TILE)]),
        (inv_high, inv.at[0]), (inv_low, inv.at[1]),
    ]
    loads = [
        pltpu.make_async_copy(source, target, load_sems.at[n]) for n, (source, target) in enumerate(pairs)
    ]
    for load in loads:
        load.start()
    for load in loads:
        load.wait()

    weighted = go[0].astype(jnp.float32) * og[0].astype(jnp.float32)
    gated = gi[0].astype(jnp.float32) * va[0].astype(jnp.float32)
    weighted = weighted.T.reshape(members, 1, ROWS, TILE)
    gated = gated.T.reshape(members, 1, ROWS, TILE)
    outgoing[...] = (
        jnp.concatenate([weighted, gated], axis=1)
        .reshape(members, 2 * ROWS, TILE)
        .astype(jnp.bfloat16)
    )
    incoming[me] = outgoing[me]

    tile = lax.broadcasted_iota(jnp.int32, docs.shape, 0)
    label = jnp.zeros(docs.shape, jnp.float32)
    end = jnp.int32(0)
    for entry in range(lengths.shape[1]):
        end = end + lengths[0, entry]
        label += (tile >= end).astype(jnp.float32)
    docs[...] = label
    spectra[pl.ds(members, ROWS)] = jnp.zeros((ROWS, 2 * ROWS, 2 * TILE), jnp.float32)
    sums[members] = jnp.zeros((ROWS, 2 * TILE), jnp.float32)

    pl.semaphore_wait(barrier, members - 1 + jnp.where(early, ring - 1, windows - 1))


    mixed_rows = [row % ring for row in (4, 1, 3, 7, 5, 2, 6, 0)][-ring:]
    mixed_rows = sorted(set(mixed_rows), key=mixed_rows.index)
    mixed = [(row, half, core) for core in range(2) for half in (1, 0) for row in mixed_rows]
    for row_step, half_step, core_step in mixed:
        if row_step + half_step + core_step == 0:
            continue
        row = lax.rem(my_row + row_step, ring)
        peer = (lax.rem(my_half + half_step, 2) * ring + row) * 2 + lax.rem(my_core + core_step, 2)
        gap = wrap(row - my_row, ring)
        number = jnp.maximum(jnp.minimum(gap, ring - gap) - 1, 0)

        remote(
            outgoing.at[peer], incoming.at[me], tile_send, tile_recv.at[number], ctx=peer
        ).start()

    @pl.when(jnp.logical_not(early))
    def _():
        for depth in range(ring // 2):
            for low in range(2):
                pl.semaphore_signal(window_sem, 1, device_id={"dp": low * ring + depth}, device_id_type=MESH)

    for number, group in enumerate(groups):
        wait_bytes(incoming.at[pl.ds(0, len(group))], tile_recv.at[number])
        places = sorted({(half, gap) for half, gap, _ in group})
        if number == 0:
            places = sorted(set(places) | {(0, 0)})
        starts = [
            (lax.rem(my_half + half, 2) * ring + lax.rem(my_row + gap, ring)) * 2 for half, gap in places
        ]
        tiles = jnp.concatenate(
            [incoming[pl.ds(start, 2)].reshape(4 * ROWS, TILE) for start in starts], axis=0
        )
        hats = product(jnp.concatenate([tiles, tiles], axis=1), fwd[...])
        for number_, start in enumerate(starts):
            spectra[pl.ds(start, 2)] = hats[number_ * 4 * ROWS : (number_ + 1) * 4 * ROWS].reshape(
                2, 2 * ROWS, 2 * TILE
            )

    def add_pairs(first, stop, terms):
        def lag_block(lag, carried):
            real = jnp.zeros((ROWS, TILE), jnp.float32)
            imag = jnp.zeros((ROWS, TILE), jnp.float32)
            for source in range(terms):
                head = source + lag
                head_real = spectra[head, :ROWS, :TILE]
                head_imag = spectra[head, :ROWS, TILE:]
                tail_real = spectra[source, ROWS:, :TILE]
                tail_imag = spectra[source, ROWS:, TILE:]
                same = docs[head] == docs[source]
                real += jnp.where(same, head_real * tail_real + head_imag * tail_imag, 0.0)
                imag += jnp.where(same, head_imag * tail_real - head_real * tail_imag, 0.0)
            sums[lag, :, :TILE] = real
            sums[lag, :, TILE:] = imag
            return carried

        lax.fori_loop(first, stop, lag_block, 0)

    quarter = members // 4
    parity = lax.broadcasted_iota(jnp.int32, (quarter * ROWS, TILE), 1) % 2
    sign = (1 - 2 * parity).astype(jnp.float32)

    def back_and_send(first):
        here = sums[pl.ds(first, quarter)].reshape(quarter * ROWS, 2 * TILE)
        after = sums[pl.ds(first + 1, quarter)].reshape(quarter * ROWS, 2 * TILE)
        both = jnp.concatenate(
            [here[:, :TILE] + sign * after[:, TILE:], here[:, TILE:] - sign * after[:, :TILE]], axis=1
        )
        high = both.astype(jnp.bfloat16)
        low = (both - high.astype(jnp.float32)).astype(jnp.bfloat16)
        result = product(high, inv[0]) + product(low, inv[0]) + product(high, inv[1])
        lags[pl.ds(first, quarter)] = result.reshape(quarter, ROWS, TILE)
        half = first // (2 * ring)
        base = lax.rem(half + my_half, 2) * ring
        for lag in range(first, first + quarter):
            slot = lag % 2
            owner = base + depth_at(half, lag // 2 % ring, me, slot, ring)

            @pl.when(owner != window)
            def _():
                remote(
                    lags.at[lag], parts.at[slot, window], lag_send, lag_recv.at[slot], dp=owner
                ).start()

    add_pairs(0, quarter + 1, members)

    @pl.when(early)
    def _():
        pl.semaphore_wait(window_sem, ring)

    back_and_send(0)
    add_pairs(quarter + 1, 2 * quarter + 1, members - quarter)
    back_and_send(quarter)
    add_pairs(2 * quarter + 1, 3 * quarter + 1, 2 * quarter)
    back_and_send(2 * quarter)
    add_pairs(3 * quarter + 1, members, quarter)
    back_and_send(3 * quarter)

    mine = [lag_of(window, me, slot, ring) for slot in range(2)]
    for slot in range(2):
        parts[slot, window] = lags[mine[slot]]
    lead = (mine[1] // 2 <= mine[0] // 2).astype(jnp.int32)

    def spread(slot, depths):
        lag = jnp.where(slot == 0, mine[0], mine[1])
        for depth in depths:
            for low in range(2):
                reader = low * ring + depth
                own = (reader == window) & (lag == me)

                @pl.when(own)
                def _():
                    pltpu.make_async_copy(total.at[slot], landing.at[me], last_recv.at[my_half]).start()

                @pl.when(jnp.logical_not(own))
                def _():
                    remote(
                        total.at[slot], landing.at[me], last_send, last_recv.at[my_half], ctx=lag, dp=reader
                    ).start()

    for slot in (lead, 1 - lead):
        wait_bytes(parts.at[slot, pl.ds(0, windows - 1)], lag_recv.at[slot])
        total[slot] = jnp.sum(parts[slot], axis=0)
        spread(slot, range(2))
    for depth in range(2, ring):
        spread(lead, [depth])
        spread(1 - lead, [depth])

    half = members // 2
    for place in range(2):
        blocks = pl.ds(place * half, half)
        wait_bytes(landing.at[blocks], last_recv.at[place])
        out[:, place * half * ROWS : (place + 1) * half * ROWS] = (
            landing[blocks].reshape(half * ROWS, TILE).T
        )

    wait_bytes(outgoing.at[pl.ds(0, members - 1)], tile_send)
    wait_bytes(lags.at[pl.ds(0, members - 2)], lag_send)
    keeps = (mine[0] == me) | (mine[1] == me)

    @pl.when(keeps)
    def _():
        wait_bytes(landing.at[pl.ds(0, members - 1)], last_send)

    @pl.when(jnp.logical_not(keeps))
    def _():
        wait_bytes(landing, last_send)


def per_device(members, windows, tables, *arrays):
    channels = members * ROWS
    hbm = pl.BlockSpec(memory_space=pltpu.HBM)
    return pl.pallas_call(
        functools.partial(kernel, members, windows),
        out_shape=pltpu.VMEM((TILE, channels), jnp.float32),
        in_specs=[hbm] * 9,
        out_specs=pl.BlockSpec(memory_space=pltpu.VMEM),
        scratch_shapes=[
            pltpu.VMEM((1, TILE, channels), jnp.bfloat16),
            pltpu.VMEM((1, TILE, channels), jnp.bfloat16),
            pltpu.VMEM((1, TILE, channels), jnp.bfloat16),
            pltpu.VMEM((1, TILE, channels), jnp.bfloat16),
            pltpu.SMEM(arrays[4].shape, jnp.int32),
            pltpu.VMEM((2 * TILE, 2 * TILE), jnp.bfloat16),
            pltpu.VMEM((2, 2 * TILE, TILE), jnp.bfloat16),
            pltpu.VMEM((members, 2 * ROWS, TILE), jnp.bfloat16),
            pltpu.VMEM((members, 2 * ROWS, TILE), jnp.bfloat16),
            pltpu.VMEM((members + ROWS, ROWS, TILE), jnp.float32),
            pltpu.VMEM((members + ROWS, 2 * ROWS, 2 * TILE), jnp.float32),
            pltpu.VMEM((members + 1, ROWS, 2 * TILE), jnp.float32),
            pltpu.VMEM((members, ROWS, TILE), jnp.float32),
            pltpu.VMEM((2, windows, ROWS, TILE), jnp.float32),
            pltpu.VMEM((2, ROWS, TILE), jnp.float32),
            pltpu.VMEM((members, ROWS, TILE), jnp.float32),
            pltpu.SemaphoreType.DMA((9,)),
            pltpu.SemaphoreType.DMA,
            pltpu.SemaphoreType.DMA((4,)),
            pltpu.SemaphoreType.DMA,
            pltpu.SemaphoreType.DMA((2,)),
            pltpu.SemaphoreType.DMA,
            pltpu.SemaphoreType.DMA((2,)),
            pltpu.SemaphoreType.REGULAR,
        ],
        compiler_params=pltpu.CompilerParams(
            collective_id=0, has_side_effects=True, vmem_limit_bytes=60 * 1024 * 1024
        ),
    )(*[pltpu.with_memory_space_constraint(array, pltpu.HBM) for array in (*arrays, *tables)])


def solution(mesh):
    members, windows = mesh.shape["ctx"], mesh.shape["dp"]
    tables = transform_tables()

    def run(*arrays):
        return per_device(members, windows, [jnp.asarray(table) for table in tables], *arrays)

    return jax.shard_map(
        run,
        mesh=mesh,
        in_specs=(P("dp", "ctx", None),) * 4 + (P("dp", None),),
        out_specs=P("ctx", None),
        check_vma=False,
    )
```

```python
import functools

import jax
import jax.numpy as jnp
import numpy as np
from jax import lax
from jax.experimental import pallas as pl
from jax.experimental.pallas import tpu as pltpu
from jax.sharding import PartitionSpec as P

TILE = 128
ROWS = 8
MESH = pl.DeviceIdType.MESH


def transform_tables():
    positions = np.arange(TILE)
    theta = 2.0 * np.pi * (np.arange(TILE) + 0.5) / (2 * TILE)
    forward = np.concatenate(
        [np.cos(positions[:, None] * theta), -np.sin(positions[:, None] * theta)], axis=1
    )
    inverse = np.concatenate(
        [np.cos(theta[:, None] * positions), -np.sin(theta[:, None] * positions)], axis=0
    )
    inverse = inverse / TILE
    split = []
    for table in (forward, inverse):
        table = table.astype(np.float32)
        high = table.astype(jnp.bfloat16)
        split += [high, (table - high.astype(np.float32)).astype(jnp.bfloat16)]
    return split


def product(left, right):
    return jnp.dot(left, right, preferred_element_type=jnp.float32)


def wrap(index, size):
    return lax.rem(index + 8 * size, size)


PLAN = [
    [
        [[2, 6, 5, 0, 4, 3, 1, 7], [4, 6, 2, 0, 7, 5, 1, 3], [7, 4, 0, 3, 1, 5, 6, 2], [3, 0, 6, 1, 2, 4, 7, 5]],
        [[6, 2, 0, 5, 1, 7, 4, 3], [7, 3, 0, 6, 5, 2, 4, 1], [0, 7, 3, 1, 5, 4, 2, 6], [2, 3, 1, 5, 4, 0, 7, 6]],
        [[3, 2, 4, 5, 7, 0, 6, 1], [1, 0, 4, 7, 6, 2, 5, 3], [5, 4, 7, 3, 1, 6, 0, 2], [6, 0, 2, 7, 3, 5, 1, 4]],
        [[3, 0, 4, 1, 7, 6, 2, 5], [2, 6, 7, 5, 1, 3, 0, 4], [5, 3, 1, 4, 2, 7, 0, 6], [6, 4, 7, 2, 5, 1, 3, 0]],
        [[3, 0, 5, 6, 2, 4, 7, 1], [0, 6, 7, 4, 3, 1, 2, 5], [1, 4, 6, 2, 3, 7, 5, 0], [4, 7, 1, 2, 6, 3, 5, 0]],
        [[1, 5, 2, 6, 7, 3, 4, 0], [1, 2, 6, 3, 7, 5, 0, 4], [0, 1, 3, 7, 4, 2, 6, 5], [4, 2, 5, 7, 3, 6, 0, 1]],
        [[2, 5, 1, 7, 4, 0, 3, 6], [5, 4, 0, 3, 7, 6, 1, 2], [4, 0, 5, 7, 6, 1, 2, 3], [0, 1, 4, 6, 5, 2, 3, 7]],
        [[7, 5, 6, 2, 1, 4, 3, 0], [5, 7, 3, 2, 1, 0, 6, 4], [6, 1, 3, 4, 5, 7, 0, 2], [0, 3, 2, 4, 6, 1, 5, 7]],
    ],
    [
        [[5, 6, 0, 2, 1, 3, 4, 7], [1, 5, 6, 3, 2, 4, 0, 7], [2, 0, 3, 7, 4, 5, 1, 6], [7, 2, 1, 6, 4, 0, 5, 3]],
        [[5, 1, 4, 7, 3, 6, 2, 0], [3, 0, 5, 4, 7, 6, 2, 1], [1, 5, 2, 6, 7, 0, 4, 3], [7, 3, 5, 4, 2, 0, 1, 6]],
        [[2, 3, 0, 7, 1, 4, 6, 5], [5, 0, 3, 1, 7, 2, 6, 4], [0, 2, 7, 5, 4, 6, 3, 1], [3, 4, 6, 2, 5, 1, 7, 0]],
        [[4, 7, 6, 2, 5, 3, 0, 1], [7, 4, 1, 6, 2, 5, 0, 3], [4, 0, 7, 2, 3, 1, 5, 6], [0, 7, 1, 3, 2, 6, 4, 5]],
        [[6, 4, 7, 2, 5, 1, 0, 3], [5, 6, 3, 7, 2, 1, 4, 0], [0, 1, 4, 5, 3, 7, 6, 2], [1, 5, 2, 3, 6, 7, 4, 0]],
        [[5, 3, 2, 7, 6, 4, 0, 1], [0, 1, 6, 5, 7, 2, 3, 4], [1, 0, 4, 7, 3, 6, 2, 5], [2, 1, 4, 3, 7, 5, 6, 0]],
        [[4, 6, 0, 3, 7, 1, 5, 2], [6, 1, 0, 4, 3, 2, 7, 5], [0, 6, 3, 4, 7, 5, 2, 1], [1, 3, 5, 7, 4, 6, 0, 2]],
        [[2, 5, 1, 6, 7, 0, 3, 4], [4, 2, 0, 5, 6, 3, 1, 7], [3, 0, 5, 7, 6, 2, 1, 4], [6, 3, 1, 7, 5, 0, 4, 2]],
    ],
]


def plan_row(half, slot, core, depth, y, ring):
    return PLAN[half][y][2 * slot + core][depth] if ring == 8 else (y + depth) % ring


def select(codes, member, ring):
    code = jnp.where(member % 2 == 0, codes[0], codes[1])
    return jnp.bitwise_and(jnp.right_shift(code, 3 * (member // 2 % ring)), 7)


def depth_at(half, row, member, slot, ring):
    codes = []
    for core in range(2):
        rows = [[plan_row(half, slot, core, depth, y, ring) for depth in range(ring)] for y in range(ring)]
        codes.append(sum(rows[y].index(row) << 3 * y for y in range(ring)))
    return select(codes, member, ring)


def lag_at(half, depth, member, slot, ring):
    codes = [
        sum(plan_row(half, slot, core, depth, y, ring) << 3 * y for y in range(ring)) for core in range(2)
    ]
    return (half * ring + select(codes, member, ring)) * 2 + slot


def lag_of(window, member, slot, ring):
    mine = lax.rem(window // ring + member // (2 * ring), 2) * ring + window % ring
    lag = lag_at(0, 0, member, slot, ring)
    for place in range(1, 2 * ring):
        lag = jnp.where(mine == place, lag_at(place // ring, place % ring, member, slot, ring), lag)
    return lag


def remote(source, target, send_sem, recv_sem, **place):
    return pltpu.make_async_remote_copy(
        src_ref=source, dst_ref=target, send_sem=send_sem, recv_sem=recv_sem,
        device_id=place, device_id_type=MESH,
    )


def wait_bytes(ref, sem):
    pltpu.make_async_copy(ref, ref, sem).wait()


def kernel(
    members, windows, out_grad, gate_out, gate_in, values, doc_tiles, fwd_high, fwd_low, inv_high, inv_low, out,
    og, go, gi, va, lengths, fwd, inv,
    outgoing, incoming, docs, spectra, sums, lags, parts, total, landing,
    load_sems, tile_send, tile_recv, lag_send, lag_recv, last_send, last_recv, window_sem,
):
    me = lax.axis_index("ctx")
    window = lax.axis_index("dp")
    ring = windows // 2
    channels = members * ROWS
    my_half, my_row, my_core = me // (2 * ring), me // 2 % ring, me % 2

    def member_at(half, row, core):
        return (lax.rem(my_half + half, 2) * ring + lax.rem(my_row + row, ring)) * 2 + lax.rem(
            my_core + core, 2
        )

    gaps = [[0] + ([1, ring - 1] if ring > 2 else [1])]
    gaps += [[gap, ring - gap] for gap in range(2, ring // 2)]
    gaps += [[ring // 2]] if ring > 2 else []
    groups = [
        [(half, gap, core) for gap in group for half in (1, 0) for core in (0, 1) if half + gap + core]
        for group in gaps
    ]
    far_first = [place for group in reversed(groups) for place in reversed(group)]

    barrier = pltpu.get_barrier_semaphore()
    for place in far_first:
        pl.semaphore_signal(barrier, 1, device_id={"ctx": member_at(*place)}, device_id_type=MESH)
    early = window % ring < ring // 2
    for depth in reversed(range(ring)):
        for low in range(2):
            known = depth >= ring // 2

            @pl.when((low * ring + depth != window) & (early | known))
            def _():
                pl.semaphore_signal(barrier, 1, device_id={"dp": low * ring + depth}, device_id_type=MESH)

    pairs = [
        (out_grad, og), (gate_out, go), (gate_in, gi), (values, va), (doc_tiles, lengths),
        (fwd_high, fwd.at[pl.ds(0, TILE)]), (fwd_low, fwd.at[pl.ds(TILE, TILE)]),
        (inv_high, inv.at[0]), (inv_low, inv.at[1]),
    ]
    loads = [
        pltpu.make_async_copy(source, target, load_sems.at[n]) for n, (source, target) in enumerate(pairs)
    ]
    for load in loads:
        load.start()
    for load in loads:
        load.wait()

    weighted = go[0].astype(jnp.float32) * og[0].astype(jnp.float32)
    gated = gi[0].astype(jnp.float32) * va[0].astype(jnp.float32)
    weighted = weighted.T.reshape(members, 1, ROWS, TILE)
    gated = gated.T.reshape(members, 1, ROWS, TILE)
    outgoing[...] = (
        jnp.concatenate([weighted, gated], axis=1)
        .reshape(members, 2 * ROWS, TILE)
        .astype(jnp.bfloat16)
    )
    incoming[me] = outgoing[me]

    tile = lax.broadcasted_iota(jnp.int32, docs.shape, 0)
    label = jnp.zeros(docs.shape, jnp.float32)
    end = jnp.int32(0)
    for entry in range(lengths.shape[1]):
        end = end + lengths[0, entry]
        label += (tile >= end).astype(jnp.float32)
    docs[...] = label
    spectra[pl.ds(members, ROWS)] = jnp.zeros((ROWS, 2 * ROWS, 2 * TILE), jnp.float32)
    sums[members] = jnp.zeros((ROWS, 2 * TILE), jnp.float32)

    pl.semaphore_wait(barrier, members - 1 + jnp.where(early, ring - 1, windows - 1))


    mixed_rows = [row % ring for row in (4, 1, 3, 7, 5, 2, 6, 0)][-ring:]
    mixed_rows = sorted(set(mixed_rows), key=mixed_rows.index)
    mixed = [(row, half, core) for half in (1, 0) for core in (1, 0) for row in mixed_rows]
    for row_step, half_step, core_step in mixed:
        if row_step + half_step + core_step == 0:
            continue
        row = lax.rem(my_row + row_step, ring)
        peer = (lax.rem(my_half + half_step, 2) * ring + row) * 2 + lax.rem(my_core + core_step, 2)
        gap = wrap(row - my_row, ring)
        number = jnp.maximum(jnp.minimum(gap, ring - gap) - 1, 0)

        remote(
            outgoing.at[peer], incoming.at[me], tile_send, tile_recv.at[number], ctx=peer
        ).start()

    @pl.when(jnp.logical_not(early))
    def _():
        for depth in range(ring // 2):
            for low in range(2):
                pl.semaphore_signal(window_sem, 1, device_id={"dp": low * ring + depth}, device_id_type=MESH)

    for number, group in enumerate(groups):
        wait_bytes(incoming.at[pl.ds(0, len(group))], tile_recv.at[number])
        places = sorted({(half, gap) for half, gap, _ in group})
        if number == 0:
            places = sorted(set(places) | {(0, 0)})
        starts = [
            (lax.rem(my_half + half, 2) * ring + lax.rem(my_row + gap, ring)) * 2 for half, gap in places
        ]
        tiles = jnp.concatenate(
            [incoming[pl.ds(start, 2)].reshape(4 * ROWS, TILE) for start in starts], axis=0
        )
        hats = product(jnp.concatenate([tiles, tiles], axis=1), fwd[...])
        for number_, start in enumerate(starts):
            spectra[pl.ds(start, 2)] = hats[number_ * 4 * ROWS : (number_ + 1) * 4 * ROWS].reshape(
                2, 2 * ROWS, 2 * TILE
            )

    def add_pairs(first, stop, terms):
        def lag_block(lag, carried):
            real = jnp.zeros((ROWS, TILE), jnp.float32)
            imag = jnp.zeros((ROWS, TILE), jnp.float32)
            for source in range(terms):
                head = source + lag
                head_real = spectra[head, :ROWS, :TILE]
                head_imag = spectra[head, :ROWS, TILE:]
                tail_real = spectra[source, ROWS:, :TILE]
                tail_imag = spectra[source, ROWS:, TILE:]
                same = docs[head] == docs[source]
                real += jnp.where(same, head_real * tail_real + head_imag * tail_imag, 0.0)
                imag += jnp.where(same, head_imag * tail_real - head_real * tail_imag, 0.0)
            sums[lag, :, :TILE] = real
            sums[lag, :, TILE:] = imag
            return carried

        lax.fori_loop(first, stop, lag_block, 0)

    quarter = members // 4
    parity = lax.broadcasted_iota(jnp.int32, (quarter * ROWS, TILE), 1) % 2
    sign = (1 - 2 * parity).astype(jnp.float32)

    def back_and_send(first):
        here = sums[pl.ds(first, quarter)].reshape(quarter * ROWS, 2 * TILE)
        after = sums[pl.ds(first + 1, quarter)].reshape(quarter * ROWS, 2 * TILE)
        both = jnp.concatenate(
            [here[:, :TILE] + sign * after[:, TILE:], here[:, TILE:] - sign * after[:, :TILE]], axis=1
        )
        high = both.astype(jnp.bfloat16)
        low = (both - high.astype(jnp.float32)).astype(jnp.bfloat16)
        result = product(high, inv[0]) + product(low, inv[0]) + product(high, inv[1])
        lags[pl.ds(first, quarter)] = result.reshape(quarter, ROWS, TILE)
        half = first // (2 * ring)
        base = lax.rem(half + my_half, 2) * ring
        for lag in range(first, first + quarter):
            slot = lag % 2
            owner = base + depth_at(half, lag // 2 % ring, me, slot, ring)

            @pl.when(owner != window)
            def _():
                remote(
                    lags.at[lag], parts.at[slot, window], lag_send, lag_recv.at[slot], dp=owner
                ).start()

    add_pairs(0, quarter + 1, members)

    @pl.when(early)
    def _():
        pl.semaphore_wait(window_sem, ring)

    back_and_send(0)
    add_pairs(quarter + 1, 2 * quarter + 1, members - quarter)
    back_and_send(quarter)
    add_pairs(2 * quarter + 1, 3 * quarter + 1, 2 * quarter)
    back_and_send(2 * quarter)
    add_pairs(3 * quarter + 1, members, quarter)
    back_and_send(3 * quarter)

    mine = [lag_of(window, me, slot, ring) for slot in range(2)]
    for slot in range(2):
        parts[slot, window] = lags[mine[slot]]
    lead = (mine[1] // 2 <= mine[0] // 2).astype(jnp.int32)

    def spread(slot, depths):
        lag = jnp.where(slot == 0, mine[0], mine[1])
        for depth in depths:
            for low in range(2):
                reader = low * ring + depth
                own = (reader == window) & (lag == me)

                @pl.when(own)
                def _():
                    pltpu.make_async_copy(total.at[slot], landing.at[me], last_recv).start()

                @pl.when(jnp.logical_not(own))
                def _():
                    remote(
                        total.at[slot], landing.at[me], last_send, last_recv, ctx=lag, dp=reader
                    ).start()

    for slot in (lead, 1 - lead):
        wait_bytes(parts.at[slot, pl.ds(0, windows - 1)], lag_recv.at[slot])
        total[slot] = jnp.sum(parts[slot], axis=0)
        spread(slot, range(2))
    for depth in range(2, ring):
        spread(lead, [depth])
        spread(1 - lead, [depth])

    wait_bytes(landing, last_recv)
    out[...] = landing[...].reshape(channels, TILE).T

    wait_bytes(outgoing.at[pl.ds(0, members - 1)], tile_send)
    wait_bytes(lags.at[pl.ds(0, members - 2)], lag_send)
    keeps = (mine[0] == me) | (mine[1] == me)

    @pl.when(keeps)
    def _():
        wait_bytes(landing.at[pl.ds(0, members - 1)], last_send)

    @pl.when(jnp.logical_not(keeps))
    def _():
        wait_bytes(landing, last_send)


def per_device(members, windows, tables, *arrays):
    channels = members * ROWS
    hbm = pl.BlockSpec(memory_space=pltpu.HBM)
    return pl.pallas_call(
        functools.partial(kernel, members, windows),
        out_shape=pltpu.VMEM((TILE, channels), jnp.float32),
        in_specs=[hbm] * 9,
        out_specs=pl.BlockSpec(memory_space=pltpu.VMEM),
        scratch_shapes=[
            pltpu.VMEM((1, TILE, channels), jnp.bfloat16),
            pltpu.VMEM((1, TILE, channels), jnp.bfloat16),
            pltpu.VMEM((1, TILE, channels), jnp.bfloat16),
            pltpu.VMEM((1, TILE, channels), jnp.bfloat16),
            pltpu.SMEM(arrays[4].shape, jnp.int32),
            pltpu.VMEM((2 * TILE, 2 * TILE), jnp.bfloat16),
            pltpu.VMEM((2, 2 * TILE, TILE), jnp.bfloat16),
            pltpu.VMEM((members, 2 * ROWS, TILE), jnp.bfloat16),
            pltpu.VMEM((members, 2 * ROWS, TILE), jnp.bfloat16),
            pltpu.VMEM((members + ROWS, ROWS, TILE), jnp.float32),
            pltpu.VMEM((members + ROWS, 2 * ROWS, 2 * TILE), jnp.float32),
            pltpu.VMEM((members + 1, ROWS, 2 * TILE), jnp.float32),
            pltpu.VMEM((members, ROWS, TILE), jnp.float32),
            pltpu.VMEM((2, windows, ROWS, TILE), jnp.float32),
            pltpu.VMEM((2, ROWS, TILE), jnp.float32),
            pltpu.VMEM((members, ROWS, TILE), jnp.float32),
            pltpu.SemaphoreType.DMA((9,)),
            pltpu.SemaphoreType.DMA,
            pltpu.SemaphoreType.DMA((4,)),
            pltpu.SemaphoreType.DMA,
            pltpu.SemaphoreType.DMA((2,)),
            pltpu.SemaphoreType.DMA,
            pltpu.SemaphoreType.DMA,
            pltpu.SemaphoreType.REGULAR,
        ],
        compiler_params=pltpu.CompilerParams(
            collective_id=0, has_side_effects=True, vmem_limit_bytes=60 * 1024 * 1024
        ),
    )(*[pltpu.with_memory_space_constraint(array, pltpu.HBM) for array in (*arrays, *tables)])


def solution(mesh):
    members, windows = mesh.shape["ctx"], mesh.shape["dp"]
    tables = transform_tables()

    def run(*arrays):
        return per_device(members, windows, [jnp.asarray(table) for table in tables], *arrays)

    return jax.shard_map(
        run,
        mesh=mesh,
        in_specs=(P("dp", "ctx", None),) * 4 + (P("dp", None),),
        out_specs=P("ctx", None),
        check_vma=False,
    )
```
